32 devices in a mesh: fsdp: 2 (over x), ctx: 4 (over z), tp: 4 (over y, core).
Axes of the slice: x: 2, y: 2, z: 4, core: 2. Of those that a mesh axis runs over, the one named last changes fastest.
Arguments:
- tokens: bfloat16 [4096, 2048], P(('fsdp', 'ctx')), may hold values from -6 to 6
- first_gain: bfloat16 [2048], P('fsdp'), may hold values from 0.099609375 to 1.8984375
- query_weight: bfloat16 [2048, 2048], P('fsdp', 'tp'), may hold values from -0.125 to 0.125
- keyval_weight: bfloat16 [2048, 512], P('fsdp', 'tp'), may hold values from -0.125 to 0.125
- output_weight: bfloat16 [2048, 2048], P('tp', 'fsdp'), may hold values from -2 to 2
- second_gain: bfloat16 [2048], P('fsdp'), may hold values from 0.099609375 to 1.8984375
- gate_weight: bfloat16 [2048, 5632], P('fsdp', 'tp'), may hold values from -0.125 to 0.125
- up_weight: bfloat16 [2048, 5632], P('fsdp', 'tp'), may hold values from -0.125 to 0.125
- down_weight: bfloat16 [5632, 2048], P('tp', 'fsdp'), may hold values from -0.078125 to 0.078125
- segment_ids: int32 [4096], P('fsdp'), may hold values from 0 to 2049, as said below
- positions: int32 [4096], P('fsdp'), may hold values from 0 to 1023, as said below
- cotangent: bfloat16 [4096, 2048], P(('fsdp', 'ctx')), may hold values from -6 to 6
Outputs:
- activations: bfloat16 [4096, 2048], P(('fsdp', 'ctx'))
- input_grad: float32 [4096, 2048], P(('fsdp', 'ctx'))
- first_gain_grad: float32 [2048], P('fsdp')
- query_grad: float32 [2048, 2048], P('fsdp', 'tp')
- keyval_grad: float32 [2048, 512], P('fsdp', 'tp')
- output_grad: float32 [2048, 2048], P('tp', 'fsdp')
- second_gain_grad: float32 [2048], P('fsdp')
- gate_grad: float32 [2048, 5632], P('fsdp', 'tp')
- up_grad: float32 [2048, 5632], P('fsdp', 'tp')
- down_grad: float32 [5632, 2048], P('tp', 'fsdp')
The draws below stay inside these ranges and needn't reach their ends.
Inputs may be any that keep to these rules, and one draw needn't show every extreme that they name: `segment_ids`: each group of 2048 slots holds 2 sequences with ids 0 to 1, one of exactly 1024 tokens, the others of 512 to 1023; every other slot is padding whose id is 2 plus its slot's place in the virtual order of the group, an id of its own; the last slot of that order is always padding. Slots come in tiles of 128; the tiles of one group lie in sequence order dealt in turn over the devices of ctx, in an order within a device drawn from the seed. The tokens of a sequence carry positions 0 to its length - 1, each once; padding slots carry 0.
All inputs are finite; a program needn't handle non-finite values.
Results may differ from the reference program's by a relative error of at most 0.014.
Values may be sent and summed in bfloat16 or wider, within the bound.
No kernel may reach another device: no remote copies, remote signals or barrier semaphores. Data moves between devices by JAX's collectives and lax.ppermute only.
A program may use at most 192 MiB of HBM per device.

```python
import math
import jax
import jax.numpy as jnp
from jax import lax

D = 2048
HEADS = 32
KV_HEADS = 4
HD = 64
FF = 5632
TOK_DEV = 512
TILE = 128
LONGEST = 1024
SHORTEST = 512
TOKENS = 4096
N_FSDP = 2
N_CTX = 4


def layout(key):
    group_rows = TOK_DEV * N_CTX
    seq_count = group_rows // LONGEST
    key_length, key_pick, key_order = jax.random.split(key, 3)
    lengths = jax.random.randint(key_length, (N_FSDP, seq_count), SHORTEST, LONGEST)
    picked = jax.random.randint(key_pick, (N_FSDP, 1), 0, seq_count)
    lengths = jnp.where(jnp.arange(seq_count)[None, :] == picked, LONGEST, lengths)
    ends = jnp.cumsum(lengths, axis=1)
    starts = ends - lengths
    slots = jnp.arange(group_rows)
    member = jnp.sum((slots[None, :, None] >= ends[:, None, :]).astype(jnp.int32), axis=2)
    inside = member < seq_count
    bounded = jnp.minimum(member, seq_count - 1)
    begins = jnp.take_along_axis(starts, bounded, axis=1)
    segment = jnp.where(inside, member, seq_count + slots[None, :])
    place = jnp.where(inside, slots[None, :] - begins, 0)
    tiles_device = TOK_DEV // TILE
    virtual_tile = slots // TILE
    device = virtual_tile % N_CTX
    order = virtual_tile // N_CTX
    order_keys = jax.random.split(key_order, N_FSDP * N_CTX)
    shuffles = jax.vmap(lambda single: jax.random.permutation(single, tiles_device))(order_keys).reshape(N_FSDP, N_CTX, tiles_device)
    local_tile = shuffles[:, device, order]
    target = device[None, :] * TOK_DEV + local_tile * TILE + (slots % TILE)[None, :]
    group_index = jnp.arange(N_FSDP)[:, None]
    segs = jnp.zeros((N_FSDP, group_rows), jnp.int32).at[group_index, target].set(segment.astype(jnp.int32))
    places = jnp.zeros((N_FSDP, group_rows), jnp.int32).at[group_index, target].set(place.astype(jnp.int32))
    return (segs.reshape(-1).astype(jnp.int32), places.reshape(-1).astype(jnp.int32))


def draw_segment_ids(key, part):
    shared = layout(key)
    return shared[0]


def draw_positions(key, part):
    shared = layout(key)
    return shared[1]


def levels(rng, dims, shards, least, high):
    loudness, own = 1.0, jax.random.fold_in(rng, 6)
    for dim, parts in shards:
        draws = jnp.exp(jax.random.uniform(jax.random.fold_in(own, dim), (parts,), jnp.float32, least / len(shards), high / len(shards)))
        loudness = loudness * jnp.repeat(draws, dims[dim] // parts).reshape([-1 if axis == dim else 1 for axis in range(len(dims))])
    return loudness


def normal_values(rng, shape, width, bound, cuts=(), held_as=jnp.bfloat16):
    drawn = jax.random.normal(rng, shape, jnp.float32) * width
    if len(cuts) > 0:
        drawn = levels(rng, shape, cuts, -0.22, 0.18) * drawn
    return jnp.clip(drawn, min=-bound, max=bound).astype(held_as)


def setup_inputs(seed: int = 0) -> dict:
    seeds = jax.random.split(jax.random.key(seed), 13)
    tokens = normal_values(seeds[0], (TOKENS, D), 1.0, 6.0, ((0, 8),))
    first_gain = jnp.clip(1.0 + 0.18 * jax.random.normal(seeds[1], (D,), jnp.float32), 0.099609375, 1.8984375).astype(jnp.bfloat16)
    query_weight = normal_values(seeds[2], (D, HEADS * HD), D ** -0.5, 0.125, ((0, 2), (1, 4)))
    keyval_weight = normal_values(seeds[3], (D, 2 * KV_HEADS * HD), D ** -0.5, 0.125, ((0, 2), (1, 4)))
    output_weight = normal_values(seeds[4], (HEADS * HD, D), (max(HEADS * HD // 256, 1)) ** -0.5, 2.0, ((0, 4), (1, 2)))
    second_gain = jnp.clip(1.0 + 0.18 * jax.random.normal(seeds[5], (D,), jnp.float32), 0.099609375, 1.8984375).astype(jnp.bfloat16)
    gate_weight = normal_values(seeds[6], (D, FF), D ** -0.5, 0.125, ((0, 2), (1, 4)))
    up_weight = normal_values(seeds[7], (D, FF), D ** -0.5, 0.125, ((0, 2), (1, 4)))
    down_weight = normal_values(seeds[8], (FF, D), FF ** -0.5, 0.078125, ((0, 4), (1, 2)))
    segment_ids = draw_segment_ids(jax.random.fold_in(seeds[12], 71), 0)
    positions = draw_positions(jax.random.fold_in(seeds[12], 71), 0)
    cotangent = normal_values(seeds[11], (TOKENS, D), 1.0, 6.0, ((0, 8),))
    return {"tokens": tokens, "first_gain": first_gain, "query_weight": query_weight, "keyval_weight": keyval_weight, "output_weight": output_weight, "second_gain": second_gain, "gate_weight": gate_weight, "up_weight": up_weight, "down_weight": down_weight, "segment_ids": segment_ids, "positions": positions, "cotangent": cotangent}


epsilon = 1e-05

@jax.custom_vjp
def low(v):
    return lax.optimization_barrier(v.astype(jnp.bfloat16)).astype(jnp.float32)

@jax.custom_vjp
def low_back(v):
    return v

def low_keep(v):
    return (low(v), None)

def low_pass(kept, grad):
    return (grad,)

def back_keep(v):
    return (v, None)

def back_low(kept, grad):
    return (low(grad),)
low.defvjp(low_keep, low_pass)
low_back.defvjp(back_keep, back_low)

def rotate(values, places):
    half = values.shape[-1] // 2
    ladder = jnp.arange(half).astype(values.dtype)
    freqs = jnp.exp(ladder * (-2.0 * math.log(10000.0) / values.shape[-1]))
    angles = places.astype(values.dtype)[:, None] * freqs[None, :]
    cosine = jnp.cos(angles)[:, None, :]
    sine = jnp.sin(angles)[:, None, :]
    former = values[..., :half]
    latter = values[..., half:]
    return jnp.concatenate([former * cosine - latter * sine, latter * cosine + former * sine], axis=-1)

def rms_norm(values, gain):
    return values * lax.rsqrt(lax.optimization_barrier(jnp.mean(values * values, axis=-1, keepdims=True)) + epsilon) * gain

def attend_block(query_block, seg_rows, place_rows, keys, values, seg_all, place_all):
    highest = lax.Precision.HIGHEST
    scores = low_back(jnp.einsum('qjgd,kjd->qjgk', query_block, keys, precision=highest) * 0.125)
    allowed = (seg_rows[:, None] == seg_all[None, :]) & (place_all[None, :] <= place_rows[:, None])
    scores = jnp.where(allowed[:, None, None, :], scores, -1e+30)
    probs = low(jax.nn.softmax(scores, axis=-1))
    return jnp.einsum('qjgk,kjd->qjgd', probs, values, precision=highest)

def layer(inputs, gain_one, w_query, w_keyval, w_output, gain_two, w_gate, w_upper, w_down, segments, places):
    highest = lax.Precision.HIGHEST
    token_rows = inputs.shape[0]
    group_size = HEADS // KV_HEADS
    normed_one = low(rms_norm(inputs, gain_one))
    query_pre = low_back(jnp.dot(normed_one, w_query, precision=highest).reshape(token_rows, HEADS, HD))
    keyval_pre = jnp.dot(normed_one, w_keyval, precision=highest).reshape(token_rows, KV_HEADS, 2, HD)
    key_pre = low_back(keyval_pre[:, :, 0])
    value_low = low(low_back(keyval_pre[:, :, 1]))
    queries = low(rotate(query_pre, places)).reshape(token_rows, KV_HEADS, group_size, HD)
    keys = low(rotate(key_pre, places))
    block_rows = min(512, token_rows)
    block_count = token_rows // block_rows

    def one_block(member):
        return attend_block(member[0], member[1], member[2], keys, value_low, segments, places)
    pieces = lax.map(jax.checkpoint(one_block), (queries.reshape(block_count, block_rows, KV_HEADS, group_size, HD), segments.reshape(block_count, block_rows), places.reshape(block_count, block_rows)))
    mixed = low(low_back(pieces.reshape(token_rows, HEADS * HD)))
    hidden_one = inputs + low_back(jnp.dot(mixed, w_output, precision=highest))
    normed_two = low(rms_norm(hidden_one, gain_two))
    gate = low_back(jnp.dot(normed_two, w_gate, precision=highest))
    upper = low_back(jnp.dot(normed_two, w_upper, precision=highest))
    hidden = low(jax.nn.silu(gate) * upper)
    return hidden_one + low_back(jnp.dot(hidden, w_down, precision=highest))

def reference(tokens, first_gain, query_weight, keyval_weight, output_weight, second_gain, gate_weight, up_weight, down_weight, segment_ids, positions, cotangent):
    weights = tuple((member.astype(jnp.float32) for member in (first_gain, query_weight, keyval_weight, output_weight, second_gain, gate_weight, up_weight, down_weight)))
    group_rows = TOK_DEV * N_CTX

    def one_group(carry, member):
        inputs, segments, places, upstream = member

        def forward(values, *params):
            return layer(values, *params, segments, places)
        outcome, pullback = jax.vjp(forward, inputs.astype(jnp.float32), *weights)
        grads = pullback(upstream.astype(jnp.float32))
        summed = tuple((total + part for total, part in zip(carry, grads[1:])))
        return (summed, (outcome.astype(jnp.bfloat16), grads[0]))
    zero_grads = tuple((jnp.zeros(member.shape, jnp.float32) for member in weights))
    stacked = (tokens.reshape(N_FSDP, group_rows, D), segment_ids.reshape(N_FSDP, group_rows), positions.reshape(N_FSDP, group_rows), cotangent.reshape(N_FSDP, group_rows, D))
    totals, (outputs, input_grads) = lax.scan(one_group, zero_grads, stacked)
    return (outputs.reshape(-1, D), input_grads.reshape(-1, D), totals[0], totals[1], totals[2], totals[3], totals[4], totals[5], totals[6], totals[7])
```

```python
import functools
import math

import jax
import jax.numpy as jnp
from jax import lax
from jax.experimental import pallas as pl
from jax.experimental.pallas import tpu as pltpu
from jax.sharding import PartitionSpec as P

HD = 64
TILE = 128
CODE = 4096
NEGATIVE = -1e30
epsilon = 1e-05
MIB = 2**20


def dot(left, right, over_left, over_right):
    return lax.dot_general(
        left,
        right,
        (((over_left,), (over_right,)), ((), ())),
        preferred_element_type=jnp.float32,
    )


def swap(value, axis, size, distance):
    pairs = [(i, i ^ distance) for i in range(size)]
    return lax.ppermute(value, axis, pairs)


def shift(value, axis, size, distance):
    pairs = [(i, (i + distance) % size) for i in range(size)]
    return lax.ppermute(value, axis, pairs)


def bit_of(axis, distance):
    return (lax.axis_index(axis) // distance) % 2


def scatter_rows(part, axis, size):
    distance = 1
    while distance < size:
        halves = part.reshape((2, part.shape[0] // 2) + part.shape[1:])
        bit = bit_of(axis, distance)
        give = lax.dynamic_index_in_dim(halves, 1 - bit, 0, False).astype(jnp.bfloat16)
        keep = lax.dynamic_index_in_dim(halves, bit, 0, False)
        part = keep.astype(jnp.float32) + swap(give, axis, size, distance).astype(jnp.float32)
        distance *= 2
    return part


def own_rows(whole, axis, size):
    distance = 1
    while distance < size:
        halves = whole.reshape((2, whole.shape[0] // 2) + whole.shape[1:])
        whole = lax.dynamic_index_in_dim(halves, bit_of(axis, distance), 0, False)
        distance *= 2
    return whole


def in_order(bit, mine, other, dim):
    return jnp.where(
        bit == 0,
        jnp.concatenate([mine, other], axis=dim),
        jnp.concatenate([other, mine], axis=dim),
    )


def gather_rows(rows, axis, size):
    distance = size // 2
    while distance >= 1:
        other = swap(rows, axis, size, distance)
        rows = in_order(bit_of(axis, distance), rows, other, 0)
        distance //= 2
    return rows


def sum_all(value, axis, size):
    distance = 1
    while distance < size:
        value = value + swap(value, axis, size, distance)
        distance *= 2
    return value


def gather_weight(shard, size, dim):
    if size != 2:
        return lax.all_gather(shard, "fsdp", axis=dim, tiled=True)
    return in_order(lax.axis_index("fsdp"), shard, swap(shard, "fsdp", 2, 1), dim)


def line_sum(pieces, size):
    if size != 4:
        return [lax.psum(piece.astype(jnp.float32), "ctx") for piece in pieces]
    place = lax.axis_index("ctx")
    inner = (place == 1) | (place == 2)
    done = []
    for piece in pieces:
        low = piece.astype(jnp.bfloat16)
        low = low + lax.ppermute(low, "ctx", [(0, 1), (3, 2)])
        low = low + lax.ppermute(low, "ctx", [(1, 2), (2, 1)])
        final = lax.ppermute(low, "ctx", [(1, 0), (2, 3)])
        done.append(jnp.where(inner, low, final).astype(jnp.float32))
    return done


def attend_kernel(
    heads, count, tiles, q, kv, q_code, q_base, k_code, mixed, lse, top, total, acc
):
    step = pl.program_id(0)
    top[...] = jnp.full_like(top, NEGATIVE)
    total[...] = jnp.zeros_like(total)
    acc[...] = jnp.zeros_like(acc)
    code, base = q_code[...], q_base[...]

    def body(j, carry):
        tile = tiles[step, j]
        keys = kv[tile, :HD]
        values = kv[tile, HD:]
        key_code = k_code[tile]
        allowed = (key_code <= code) & (key_code >= base)
        for h in range(heads):
            scores = jnp.where(allowed, dot(keys, q[h], 0, 0), NEGATIVE)
            before = top[h : h + 1]
            highest = jnp.maximum(before, jnp.max(scores, axis=0, keepdims=True))
            probs = jnp.exp(scores - highest)
            fade = jnp.exp(before - highest)
            top[h : h + 1] = highest
            total[h : h + 1] = total[h : h + 1] * fade + jnp.sum(probs, axis=0, keepdims=True)
            acc[h] = acc[h] * fade + dot(values, probs.astype(jnp.bfloat16), 1, 0)
        return carry

    lax.fori_loop(0, count[step], body, 0)
    sums = total[...]
    lse[...] = top[...] + jnp.log(sums)
    inverse = 1.0 / sums
    for h in range(heads):
        mixed[h] = acc[h] * inverse[h : h + 1]


def attend(count, tiles, q, kv, q_code, q_base, k_code):
    heads, _, rows = q.shape
    stack = pl.BlockSpec(kv.shape, lambda i, *_: (0, 0, 0))
    codes = pl.BlockSpec(k_code.shape, lambda i, *_: (0, 0, 0))
    line = pl.BlockSpec((1, TILE), lambda i, *_: (0, i))
    block = pl.BlockSpec((heads, HD, TILE), lambda i, *_: (0, 0, i))
    return pl.pallas_call(
        functools.partial(attend_kernel, heads),
        grid_spec=pltpu.PrefetchScalarGridSpec(
            num_scalar_prefetch=2,
            grid=(rows // TILE,),
            in_specs=[block, stack, line, line, codes],
            out_specs=[block, pl.BlockSpec((heads, TILE), lambda i, *_: (0, i))],
            scratch_shapes=[
                pltpu.VMEM((heads, TILE), jnp.float32),
                pltpu.VMEM((heads, TILE), jnp.float32),
                pltpu.VMEM((heads, HD, TILE), jnp.float32),
            ],
        ),
        out_shape=[
            jax.ShapeDtypeStruct((heads, HD, rows), jnp.float32),
            jax.ShapeDtypeStruct((heads, rows), jnp.float32),
        ],
        compiler_params=pltpu.CompilerParams(vmem_limit_bytes=32 * MIB),
        cost_estimate=pl.CostEstimate(
            flops=10 * 10**9, bytes_accessed=4 * MIB, transcendentals=4 * MIB
        ),
    )(count, tiles, q, kv, q_code, q_base, k_code)


def attend_back_kernel(
    heads, count, tiles, q, kv, q_code, q_base, k_code, mixed, lse, upstream, dq, dkv, centre
):
    step = pl.program_id(0)

    @pl.when(step == 0)
    def _():
        dkv[...] = jnp.zeros_like(dkv)

    dq[...] = jnp.zeros_like(dq)
    code, base = q_code[...], q_base[...]
    for h in range(heads):
        centre[h : h + 1] = jnp.sum(
            mixed[h] * upstream[h].astype(jnp.float32), axis=0, keepdims=True
        )

    def body(j, carry):
        tile = tiles[step, j]
        keys = kv[tile, :HD]
        values = kv[tile, HD:]
        key_code = k_code[tile]
        allowed = (key_code <= code) & (key_code >= base)
        key_term = dkv[tile, :HD]
        value_term = dkv[tile, HD:]
        for h in range(heads):
            scores = dot(keys, q[h], 0, 0) - lse[h : h + 1]
            probs = jnp.exp(jnp.where(allowed, scores, NEGATIVE))
            grad_probs = dot(values, upstream[h], 0, 0)
            grad_scores = (probs * (grad_probs - centre[h : h + 1])).astype(jnp.bfloat16)
            value_term = value_term + dot(upstream[h], probs.astype(jnp.bfloat16), 1, 1)
            key_term = key_term + dot(q[h], grad_scores, 1, 1)
            dq[h] += dot(keys, grad_scores, 1, 0)
        dkv[tile, :HD] = key_term
        dkv[tile, HD:] = value_term
        return carry

    lax.fori_loop(0, count[step], body, 0)


def attend_back(count, tiles, q, kv, q_code, q_base, k_code, mixed, lse, upstream):
    heads, _, rows = q.shape
    stack = pl.BlockSpec(kv.shape, lambda i, *_: (0, 0, 0))
    codes = pl.BlockSpec(k_code.shape, lambda i, *_: (0, 0, 0))
    line = pl.BlockSpec((1, TILE), lambda i, *_: (0, i))
    block = pl.BlockSpec((heads, HD, TILE), lambda i, *_: (0, 0, i))
    return pl.pallas_call(
        functools.partial(attend_back_kernel, heads),
        grid_spec=pltpu.PrefetchScalarGridSpec(
            num_scalar_prefetch=2,
            grid=(rows // TILE,),
            in_specs=[
                block,
                stack,
                line,
                line,
                codes,
                block,
                pl.BlockSpec((heads, TILE), lambda i, *_: (0, i)),
                block,
            ],
            out_specs=[block, stack],
            scratch_shapes=[pltpu.VMEM((heads, TILE), jnp.float32)],
        ),
        out_shape=[
            jax.ShapeDtypeStruct((heads, HD, rows), jnp.float32),
            jax.ShapeDtypeStruct(kv.shape, jnp.float32),
        ],
        compiler_params=pltpu.CompilerParams(vmem_limit_bytes=32 * MIB),
        cost_estimate=pl.CostEstimate(
            flops=30 * 10**9, bytes_accessed=6 * MIB, transcendentals=4 * MIB
        ),
    )(count, tiles, q, kv, q_code, q_base, k_code, mixed, lse, upstream)


def plan_tiles(q_code, q_base, k_code):
    rows, keys = q_code.shape[0], k_code.shape[0]
    allowed = (k_code[None, :] <= q_code[:, None]) & (k_code[None, :] >= q_base[:, None])
    used = jnp.any(allowed.reshape(rows // TILE, TILE, keys // TILE, TILE), axis=(1, 3))
    place = jnp.cumsum(used.astype(jnp.int32), axis=1) - 1
    ladder = jnp.arange(keys // TILE)
    hit = used[:, :, None] & (place[:, :, None] == ladder[None, None, :])
    tiles = jnp.sum(jnp.where(hit, ladder[None, :, None], 0), axis=1).astype(jnp.int32)
    return jnp.sum(used.astype(jnp.int32), axis=1), tiles


def middle_kernel(rows, upstream, gate_w, upper_w, down_w, hidden, dgate, dupper):
    gate = dot(rows[...], gate_w[...], 1, 0)
    upper = dot(rows[...], upper_w[...], 1, 0)
    grad = dot(upstream[...], down_w[...], 1, 1)
    sigma = 1.0 / (1.0 + jnp.exp(-gate))
    swish = gate * sigma
    hidden[...] = (swish * upper).astype(jnp.bfloat16)
    dgate[...] = (grad * upper * sigma * (1.0 + gate * (1.0 - sigma))).astype(jnp.bfloat16)
    dupper[...] = (grad * swish).astype(jnp.bfloat16)


def middle(rows, upstream, gate_w, upper_w, down_w):
    count, width = rows.shape
    units = gate_w.shape[1]
    block = 256
    whole = pl.BlockSpec((count, width), lambda i: (0, 0))
    tall = pl.BlockSpec((width, block), lambda i: (0, i))
    out = pl.BlockSpec((count, block), lambda i: (0, i))
    return pl.pallas_call(
        middle_kernel,
        grid=(pl.cdiv(units, block),),
        in_specs=[whole, whole, tall, tall, pl.BlockSpec((block, width), lambda i: (i, 0))],
        out_specs=[out, out, out],
        out_shape=[jax.ShapeDtypeStruct((count, units), jnp.bfloat16)] * 3,
        compiler_params=pltpu.CompilerParams(vmem_limit_bytes=40 * MIB),
        cost_estimate=pl.CostEstimate(
            flops=6 * count * width * units,
            bytes_accessed=6 * width * units + 4 * count * width + 6 * count * units,
            transcendentals=count * units,
        ),
    )(rows, upstream, gate_w, upper_w, down_w)


def rms_scale(values):
    return lax.rsqrt(jnp.mean(values * values, axis=-1, keepdims=True) + epsilon)


def norm_back(values, scale, gain, upstream):
    weighted = upstream * gain
    return scale * weighted - values * scale**3 * jnp.mean(
        values * weighted, axis=-1, keepdims=True
    )


def turn(values, cosine, sine):
    half = HD // 2
    former, latter = values[:, :half], values[:, half:]
    return jnp.concatenate(
        [former * cosine - latter * sine, latter * cosine + former * sine], axis=1
    )


def per_device(
    sizes,
    tokens,
    first_gain,
    query_weight,
    keyval_weight,
    output_weight,
    second_gain,
    gate_weight,
    up_weight,
    down_weight,
    segment_ids,
    positions,
    cotangent,
):
    nx, nz, nt = sizes
    low, high = jnp.bfloat16, jnp.float32
    rows, width = tokens.shape
    half = width // nx
    here_x = lax.axis_index("fsdp")
    here_z = lax.axis_index("ctx")
    paired = nx == 2

    def mine(whole):
        return lax.dynamic_slice_in_dim(whole, here_x * half, half, 1)

    def theirs(whole):
        return lax.dynamic_slice_in_dim(whole, (1 - here_x) * half, half, 1)

    heads = query_weight.shape[1] // HD
    pairs_low = keyval_weight.shape[1] // (2 * HD)
    assert pairs_low == 1
    query_width = heads * HD
    qkv_w = gather_weight(jnp.concatenate([query_weight, keyval_weight], axis=1), nx, 0)
    gains = gather_weight(jnp.stack([first_gain, second_gain]), nx, 1).astype(high)
    output_w = gather_weight(output_weight, nx, 1)
    gate_w = gather_weight(gate_weight, nx, 0)
    upper_w = gather_weight(up_weight, nx, 0)
    down_w = gather_weight(down_weight, nx, 1)
    gain_one, gain_two = gains[0], gains[1]

    codes = (segment_ids * CODE + positions).reshape(nz, rows)
    bases = (segment_ids * CODE).reshape(nz, rows)
    q_code = lax.dynamic_index_in_dim(codes, here_z, 0, False)
    q_base = lax.dynamic_index_in_dim(bases, here_z, 0, False)
    k_code = jnp.concatenate(
        [
            lax.dynamic_index_in_dim(codes, (here_z + nz - d) % nz, 0, False)
            for d in range(nz)
        ]
    )
    count, tiles = plan_tiles(q_code, q_base, k_code)
    k_wide = jnp.broadcast_to(k_code.reshape(-1, TILE, 1), (nz * rows // TILE, TILE, TILE))
    masks = (q_code[None], q_base[None], k_wide)
    places = (q_code - q_base).astype(high)
    freqs = jnp.exp(jnp.arange(HD // 2).astype(high) * (-2.0 * math.log(10000.0) / HD))
    angles = freqs[:, None] * places[None, :]
    cosine, sine = jnp.cos(angles)[None], jnp.sin(angles)[None]

    inputs = tokens.astype(high)
    scale_one = rms_scale(inputs)
    normed_one = (inputs * scale_one * gain_one).astype(low)
    qkv = dot(qkv_w, normed_one, 0, 1)
    q = turn(qkv[:query_width].reshape(heads, HD, rows), cosine, sine).astype(low) * 0.125
    k = turn(qkv[query_width : query_width + HD][None], cosine, sine)[0].astype(low)
    kv = jnp.concatenate([k, qkv[query_width + HD :].astype(low)], axis=0)
    kv = jnp.transpose(kv.reshape(2 * HD, rows // TILE, TILE), (1, 0, 2))
    kv = jnp.concatenate(
        [kv] + [shift(kv, "ctx", nz, d) for d in range(1, nz)], axis=0
    )

    mixed, lse = attend(count, tiles, q, kv, *masks)
    mixed_low = mixed.reshape(query_width, rows).astype(low)
    attn_own = scatter_rows(dot(mixed_low, output_w, 0, 0), "tp", nt)
    inputs_own = own_rows(tokens, "tp", nt).astype(high)
    upstream_low = own_rows(cotangent, "tp", nt)
    upstream_own = upstream_low.astype(high)
    one_own = inputs_own + attn_own
    scale_two = rms_scale(one_own)
    normed_own = (one_own * scale_two * gain_two).astype(low)
    normed_two = gather_rows(normed_own, "tp", nt)

    hidden, dgate, dupper = middle(normed_two, cotangent, gate_w, upper_w, down_w)
    grad_part = dot(dgate, gate_w, 1, 1) + dot(dupper, upper_w, 1, 1)
    grad_own = scatter_rows(grad_part, "tp", nt)
    ffn_own = scatter_rows(dot(hidden, down_w, 1, 0), "tp", nt)
    activations = gather_rows((one_own + ffn_own).astype(low), "tp", nt)
    gain_two_sum = jnp.sum(grad_own * one_own * scale_two, axis=0)
    grad_one = upstream_own + norm_back(one_own, scale_two, gain_two, grad_own)
    grad_attn = gather_rows(grad_one.astype(low), "tp", nt)

    if paired:
        there_cot = gather_rows(swap(upstream_low, "fsdp", 2, 1), "tp", nt)
        there_two = gather_rows(swap(normed_own, "fsdp", 2, 1), "tp", nt)
        hidden_there, dgate_there, dupper_there = middle(
            there_two, there_cot, gate_w, upper_w, down_w
        )
        down_grad = dot(hidden, mine(cotangent), 0, 0) + dot(
            hidden_there, mine(there_cot), 0, 0
        )
        left, left_there = mine(normed_two), mine(there_two)
        gate_grad = dot(left, dgate, 0, 0) + dot(left_there, dgate_there, 0, 0)
        upper_grad = dot(left, dupper, 0, 0) + dot(left_there, dupper_there, 0, 0)
        output_grad = dot(mixed_low, mine(grad_attn), 1, 0) + dot(
            swap(mixed_low, "fsdp", 2, 1), swap(theirs(grad_attn), "fsdp", 2, 1), 1, 0
        )
    else:
        down_grad = lax.psum_scatter(
            dot(hidden, cotangent, 0, 0), "fsdp", scatter_dimension=1, tiled=True
        )
        gate_grad = lax.psum_scatter(
            dot(normed_two, dgate, 0, 0), "fsdp", scatter_dimension=0, tiled=True
        )
        upper_grad = lax.psum_scatter(
            dot(normed_two, dupper, 0, 0), "fsdp", scatter_dimension=0, tiled=True
        )
        output_grad = lax.psum_scatter(
            dot(mixed_low, grad_attn, 1, 0), "fsdp", scatter_dimension=1, tiled=True
        )

    grad_mixed = dot(output_w, grad_attn, 1, 1).astype(low).reshape(heads, HD, rows)
    dq, dkv = attend_back(count, tiles, q, kv, *masks, mixed, lse, grad_mixed)
    per = rows // TILE
    dkv_own = dkv[:per]
    for d in range(1, nz):
        dkv_own = dkv_own + shift(
            dkv[d * per : (d + 1) * per].astype(low), "ctx", nz, nz - d
        ).astype(high)
    dkv_own = jnp.transpose(dkv_own, (1, 0, 2)).reshape(2 * HD, rows)
    dq = turn(dq * 0.125, cosine, -sine).reshape(query_width, rows)
    dk = turn(dkv_own[None, :HD], cosine, -sine)[0]
    dqkv = jnp.concatenate([dq, dk, dkv_own[HD:]], axis=0).astype(low)
    first_own = scatter_rows(dot(dqkv, qkv_w, 0, 1), "tp", nt)
    if paired:
        there_one = swap(theirs(normed_one), "fsdp", 2, 1)
        qkv_grad = dot(mine(normed_one), dqkv, 0, 1) + dot(
            there_one, swap(dqkv, "fsdp", 2, 1), 0, 1
        )
    else:
        qkv_grad = lax.psum_scatter(
            dot(normed_one, dqkv, 0, 1), "fsdp", scatter_dimension=0, tiled=True
        )
    scale_own = rms_scale(inputs_own)
    gain_one_sum = jnp.sum(first_own * inputs_own * scale_own, axis=0)
    input_own = grad_one + norm_back(inputs_own, scale_own, gain_one, first_own)
    input_grad = gather_rows(input_own.astype(low), "tp", nt).astype(high)

    sums = sum_all(jnp.stack([gain_one_sum, gain_two_sum]), "tp", nt)
    if paired:
        sums = mine(sums) + swap(theirs(sums), "fsdp", 2, 1)
    else:
        sums = lax.psum_scatter(sums, "fsdp", scatter_dimension=1, tiled=True)
    sums = sum_all(sums, "ctx", nz)
    down_grad, gate_grad, upper_grad, output_grad, qkv_grad = line_sum(
        [down_grad, gate_grad, upper_grad, output_grad, qkv_grad], nz
    )
    return (
        activations,
        input_grad,
        sums[0],
        qkv_grad[:, :query_width],
        qkv_grad[:, query_width:],
        output_grad,
        sums[1],
        gate_grad,
        upper_grad,
        down_grad,
    )


def solution(mesh):
    placed = (
        P(("fsdp", "ctx"), None),
        P("fsdp"),
        P("fsdp", "tp"),
        P("fsdp", "tp"),
        P("tp", "fsdp"),
        P("fsdp"),
        P("fsdp", "tp"),
        P("fsdp", "tp"),
        P("tp", "fsdp"),
        P("fsdp"),
        P("fsdp"),
        P(("fsdp", "ctx"), None),
    )
    sizes = (mesh.shape["fsdp"], mesh.shape["ctx"], mesh.shape["tp"])
    return jax.shard_map(
        functools.partial(per_device, sizes),
        mesh=mesh,
        in_specs=placed,
        out_specs=(
            P(("fsdp", "ctx"), None),
            P(("fsdp", "ctx"), None),
            P("fsdp"),
            P("fsdp", "tp"),
            P("fsdp", "tp"),
            P("tp", "fsdp"),
            P("fsdp"),
            P("fsdp", "tp"),
            P("fsdp", "tp"),
            P("tp", "fsdp"),
        ),
        check_vma=False,
    )
```

```python
import functools
import math

import jax
import jax.numpy as jnp
from jax import lax
from jax.experimental import pallas as pl
from jax.experimental.pallas import tpu as pltpu
from jax.sharding import PartitionSpec as P

HD = 64
TILE = 128
CODE = 4096
NEGATIVE = -1e30
epsilon = 1e-05
MIB = 2**20
SMALL = pl.CostEstimate(flops=1000000, bytes_accessed=100000, transcendentals=0)


def cost(microseconds):
    return pl.CostEstimate(
        flops=1000000, bytes_accessed=int(microseconds * SCALE * 3.69e6), transcendentals=0
    )


SCALE = 0.5


def dot(left, right, over_left, over_right):
    return lax.dot_general(
        left,
        right,
        (((over_left,), (over_right,)), ((), ())),
        preferred_element_type=jnp.float32,
    )


ORDER = (0, 2, 1, 3)


def swap(value, axis, distance, size):
    pairs = [(i, i ^ distance) for i in range(size)]
    return lax.ppermute(value, axis, pairs)


def shift(value, axis, size, distance):
    pairs = [(i, (i + distance) % size) for i in range(size)]
    return lax.ppermute(value, axis, pairs)


def over_x(value):
    return swap(value, "fsdp", 1, 2)


def over_y(value):
    return swap(value, "tp", 2, 4)


def over_core(value):
    return swap(value, "tp", 1, 4)


def add(left, right):
    return left.astype(jnp.float32) + right.astype(jnp.float32)


def cut(value, axis=0):
    keep, give = jnp.split(value, 2, axis=axis)
    return keep, give.astype(jnp.bfloat16)


def scatter_rows(keep, give, *tokens):
    part = add(keep, over_core(give)).astype(jnp.bfloat16)
    if part.shape[0] == 1:
        keep, give = cut(part[0])
        if tokens:
            (give,) = after([give], *tokens)
        return add(keep, over_y(give)), [give]
    left, right = jnp.split(part, 2, axis=2)
    keep_left, give_left = cut(left)
    keep_right, give_right = cut(right, 1)
    from_x, from_y = over_x(give_left), over_y(give_right)
    if tokens:
        from_x, from_y = after([from_x, from_y], *tokens)
    left = add(keep_left, from_x)[0]
    right = add(keep_right, from_y)
    keep_left, give_left = cut(left)
    keep_right, give_right = cut(right)
    left = add(keep_left, over_y(give_left))
    right = add(keep_right, over_x(give_right))[0]
    return jnp.concatenate([left, right], axis=1), [give_left, give_right]


def gather_own(rows, *tokens):
    first = jnp.concatenate([rows, over_y(rows)], axis=0)
    if tokens:
        (first,) = after([first], *tokens)
    return first, over_core(first)


def gather_pair(rows, *tokens):
    left, right = jnp.split(rows, 2, axis=1)
    left = jnp.stack([left, over_x(left)])
    right = jnp.concatenate([right, over_y(right)], axis=0)
    left = jnp.concatenate([left, over_y(left)], axis=1)
    right = jnp.stack([right, over_x(right)])
    first = jnp.concatenate([left, right], axis=2)
    if tokens:
        (first,) = after([first], *tokens)
    return first, over_core(first)


def sum_all(value, axis, size):
    distance = 1
    while distance < size:
        value = value + swap(value, axis, distance, size)
        distance *= 2
    return value


class Line:
    def __init__(self):
        self.came, self.total, self.done = [], [], []

    def put(self, piece):
        if self.came:
            earlier = (*self.came[-1:], *self.total[-2:-1], *self.done[-3:-2])
            (piece,) = after([piece], *earlier)
        self.came.append(lax.ppermute(piece, "ctx", [(0, 1), (3, 2)]))
        inward = piece + self.came[-1]
        self.total.append(inward + lax.ppermute(inward, "ctx", [(1, 2), (2, 1)]))
        self.done.append(lax.ppermute(self.total[-1], "ctx", [(1, 0), (2, 3)]))
        return len(self.total) - 1


def attend_kernel(
    heads, count, tiles, q, kv, q_code, q_base, k_code, mixed, lse, top, total, acc
):
    step = pl.program_id(0)
    top[...] = jnp.full_like(top, NEGATIVE)
    total[...] = jnp.zeros_like(total)
    acc[...] = jnp.zeros_like(acc)
    code, base = q_code[...], q_base[...]

    def body(j, carry):
        tile = tiles[step, j]
        keys = kv[tile, :HD]
        values = kv[tile, HD:]
        key_code = k_code[tile]
        allowed = (key_code <= code) & (key_code >= base)
        for h in range(heads):
            scores = jnp.where(allowed, dot(keys, q[h], 0, 0), NEGATIVE)
            before = top[h : h + 1]
            highest = jnp.maximum(before, jnp.max(scores, axis=0, keepdims=True))
            probs = jnp.exp(scores - highest)
            fade = jnp.exp(before - highest)
            top[h : h + 1] = highest
            total[h : h + 1] = total[h : h + 1] * fade + jnp.sum(probs, axis=0, keepdims=True)
            acc[h] = acc[h] * fade + dot(values, probs.astype(jnp.bfloat16), 1, 0)
        return carry

    lax.fori_loop(0, count[step], body, 0)
    sums = total[...]
    lse[...] = top[...] + jnp.log(sums)
    inverse = 1.0 / sums
    for h in range(heads):
        mixed[h] = acc[h] * inverse[h : h + 1]


def attend(count, tiles, q, kv, q_code, q_base, k_code):
    heads, _, rows = q.shape
    stack = pl.BlockSpec(kv.shape, lambda i, *_: (0, 0, 0))
    codes = pl.BlockSpec(k_code.shape, lambda i, *_: (0, 0, 0))
    line = pl.BlockSpec((1, TILE), lambda i, *_: (0, i))
    block = pl.BlockSpec((heads, HD, TILE), lambda i, *_: (0, 0, i))
    return pl.pallas_call(
        functools.partial(attend_kernel, heads),
        grid_spec=pltpu.PrefetchScalarGridSpec(
            num_scalar_prefetch=2,
            grid=(rows // TILE,),
            in_specs=[block, stack, line, line, codes],
            out_specs=[block, pl.BlockSpec((heads, TILE), lambda i, *_: (0, i))],
            scratch_shapes=[
                pltpu.VMEM((heads, TILE), jnp.float32),
                pltpu.VMEM((heads, TILE), jnp.float32),
                pltpu.VMEM((heads, HD, TILE), jnp.float32),
            ],
        ),
        out_shape=[
            jax.ShapeDtypeStruct((heads, HD, rows), jnp.float32),
            jax.ShapeDtypeStruct((heads, rows), jnp.float32),
        ],
        compiler_params=pltpu.CompilerParams(vmem_limit_bytes=60 * MIB),
        cost_estimate=SMALL,
    )(count, tiles, q, kv, q_code, q_base, k_code)


def attend_back_kernel(
    heads, count, tiles, q, kv, q_code, q_base, k_code, mixed, lse, upstream, dq, dkv, centre
):
    step = pl.program_id(0)

    @pl.when(step == 0)
    def _():
        dkv[...] = jnp.zeros_like(dkv)

    dq[...] = jnp.zeros_like(dq)
    code, base = q_code[...], q_base[...]
    for h in range(heads):
        centre[h : h + 1] = jnp.sum(
            mixed[h] * upstream[h].astype(jnp.float32), axis=0, keepdims=True
        )

    def body(j, carry):
        tile = tiles[step, j]
        keys = kv[tile, :HD]
        values = kv[tile, HD:]
        key_code = k_code[tile]
        allowed = (key_code <= code) & (key_code >= base)
        key_term = dkv[tile, :HD]
        value_term = dkv[tile, HD:]
        for h in range(heads):
            scores = dot(keys, q[h], 0, 0) - lse[h : h + 1]
            probs = jnp.exp(jnp.where(allowed, scores, NEGATIVE))
            grad_probs = dot(values, upstream[h], 0, 0)
            grad_scores = (probs * (grad_probs - centre[h : h + 1])).astype(jnp.bfloat16)
            value_term = value_term + dot(upstream[h], probs.astype(jnp.bfloat16), 1, 1)
            key_term = key_term + dot(q[h], grad_scores, 1, 1)
            dq[h] += dot(keys, grad_scores, 1, 0)
        dkv[tile, :HD] = key_term
        dkv[tile, HD:] = value_term
        return carry

    lax.fori_loop(0, count[step], body, 0)


def attend_back(count, tiles, q, kv, q_code, q_base, k_code, mixed, lse, upstream):
    heads, _, rows = q.shape
    stack = pl.BlockSpec(kv.shape, lambda i, *_: (0, 0, 0))
    codes = pl.BlockSpec(k_code.shape, lambda i, *_: (0, 0, 0))
    line = pl.BlockSpec((1, TILE), lambda i, *_: (0, i))
    block = pl.BlockSpec((heads, HD, TILE), lambda i, *_: (0, 0, i))
    return pl.pallas_call(
        functools.partial(attend_back_kernel, heads),
        grid_spec=pltpu.PrefetchScalarGridSpec(
            num_scalar_prefetch=2,
            grid=(rows // TILE,),
            in_specs=[
                block,
                stack,
                line,
                line,
                codes,
                block,
                pl.BlockSpec((heads, TILE), lambda i, *_: (0, i)),
                block,
            ],
            out_specs=[block, stack],
            scratch_shapes=[pltpu.VMEM((heads, TILE), jnp.float32)],
        ),
        out_shape=[
            jax.ShapeDtypeStruct((heads, HD, rows), jnp.float32),
            jax.ShapeDtypeStruct(kv.shape, jnp.float32),
        ],
        compiler_params=pltpu.CompilerParams(vmem_limit_bytes=60 * MIB),
        cost_estimate=cost(24),
    )(count, tiles, q, kv, q_code, q_base, k_code, mixed, lse, upstream)


def plan_tiles(q_code, q_base, k_code):
    rows, keys = q_code.shape[0], k_code.shape[0]
    allowed = (k_code[None, :] <= q_code[:, None]) & (k_code[None, :] >= q_base[:, None])
    used = jnp.any(allowed.reshape(rows // TILE, TILE, keys // TILE, TILE), axis=(1, 3))
    place = jnp.cumsum(used.astype(jnp.int32), axis=1) - 1
    ladder = jnp.arange(keys // TILE)
    hit = used[:, :, None] & (place[:, :, None] == ladder[None, None, :])
    tiles = jnp.sum(jnp.where(hit, ladder[None, :, None], 0), axis=1).astype(jnp.int32)
    return jnp.sum(used.astype(jnp.int32), axis=1), tiles


def nothing(*refs):
    pass


def after(values, *tokens):
    anywhere = pl.BlockSpec(memory_space=pl.ANY)
    return pl.pallas_call(
        nothing,
        in_specs=[anywhere] * (len(values) + len(tokens)),
        out_specs=[anywhere] * len(values),
        out_shape=[jax.ShapeDtypeStruct(v.shape, v.dtype) for v in values],
        input_output_aliases={i: i for i in range(len(values))},
    )(*values, *tokens)


def outer_kernel(parts, places, upstream, *refs):
    pieces, out = refs[:parts], refs[parts]
    total = 0.0
    for i in range(parts):
        columns = pl.ds(pl.multiple_of(places[i], TILE), pieces[i].shape[1])
        total = total + dot(upstream[:, columns], pieces[i][...], 1, 1)
    out[...] = total


def outer(places, upstream, down_w):
    count, width = upstream.shape
    units = down_w[0].shape[0]
    block = 256
    flat = [pl.BlockSpec((block, w.shape[1]), lambda i, *_: (i, 0)) for w in down_w]
    return pl.pallas_call(
        functools.partial(outer_kernel, len(down_w)),
        grid_spec=pltpu.PrefetchScalarGridSpec(
            num_scalar_prefetch=1,
            grid=(pl.cdiv(units, block),),
            in_specs=[pl.BlockSpec((count, width), lambda i, *_: (0, 0)), *flat],
            out_specs=pl.BlockSpec((count, block), lambda i, *_: (0, i)),
        ),
        out_shape=jax.ShapeDtypeStruct((count, units), jnp.float32),
        compiler_params=pltpu.CompilerParams(vmem_limit_bytes=60 * MIB),
        cost_estimate=SMALL,
    )(places, upstream, *down_w)


def middle_kernel(parts, places, rows, grads, *refs):
    pieces, (hidden, dgate, dupper) = refs[: 2 * parts], refs[2 * parts :]
    gate = upper = 0.0
    for i in range(parts):
        columns = pl.ds(pl.multiple_of(places[i], TILE), pieces[i].shape[0])
        left = rows[:, columns]
        gate = gate + dot(left, pieces[i][...], 1, 0)
        upper = upper + dot(left, pieces[parts + i][...], 1, 0)
    grad = grads[...]
    sigma = 1.0 / (1.0 + jnp.exp(-gate))
    swish = gate * sigma
    hidden[...] = (swish * upper).astype(jnp.bfloat16)
    dgate[...] = (grad * upper * sigma * (1.0 + gate * (1.0 - sigma))).astype(jnp.bfloat16)
    dupper[...] = (grad * swish).astype(jnp.bfloat16)


def middle(places, rows, grads, gate_w, upper_w):
    parts = len(gate_w)
    count, width = rows.shape
    units = gate_w[0].shape[1]
    block = 256
    out = pl.BlockSpec((count, block), lambda i, *_: (0, i))
    tall = [pl.BlockSpec((w.shape[0], block), lambda i, *_: (0, i)) for w in gate_w]
    return pl.pallas_call(
        functools.partial(middle_kernel, parts),
        grid_spec=pltpu.PrefetchScalarGridSpec(
            num_scalar_prefetch=1,
            grid=(pl.cdiv(units, block),),
            in_specs=[pl.BlockSpec((count, width), lambda i, *_: (0, 0)), out, *tall, *tall],
            out_specs=[out, out, out],
        ),
        out_shape=[jax.ShapeDtypeStruct((count, units), jnp.bfloat16)] * 3,
        compiler_params=pltpu.CompilerParams(vmem_limit_bytes=60 * MIB),
        cost_estimate=cost(9),
    )(places, rows, grads, *gate_w, *upper_w)


def project_kernel(parts, factors, steps, over_left, over_right, skip, places, *refs):
    lefts, pieces, out = refs[:factors], refs[factors:-1], refs[-1]
    step = pl.program_id(0)

    def one(i, start):
        total = 0.0
        for f in range(factors):
            left, right = lefts[f], pieces[f * parts + i]
            left = left[:, start:] if over_left else left[start:]
            right = right[:, start:] if over_right else right[start:]
            total = total + dot(left, right, over_left, over_right)
        out[...] = total.astype(out.dtype)

    for i in range(parts):
        here = (step >= i * steps) & (step < (i + 1) * steps)
        if skip:
            pl.when(here & (places[parts] == 0))(functools.partial(one, i, 0))
            pl.when(here & (places[parts] != 0))(functools.partial(one, i, skip))
        else:
            pl.when(here)(functools.partial(one, i, 0))


def project(places, lefts, weights, over_left, over_right, skip=0):
    parts, factors = len(weights[0]), len(lefts)
    axis = 1 - over_right
    size = weights[0][0].shape[axis]
    block = min(512, size)
    steps = size // block
    depth = weights[0][0].shape[over_right]
    count = lefts[0].shape[1 - over_left]

    def spec(i):
        at = lambda s: jnp.clip(s - i * steps, 0, steps - 1)
        if axis == 0:
            return pl.BlockSpec((block, depth), lambda s, *_: (at(s), 0))
        return pl.BlockSpec((depth, block), lambda s, *_: (0, at(s)))

    return pl.pallas_call(
        functools.partial(
            project_kernel, parts, factors, steps, over_left, over_right, skip
        ),
        grid_spec=pltpu.PrefetchScalarGridSpec(
            num_scalar_prefetch=1,
            grid=(parts * steps,),
            in_specs=[pl.BlockSpec(v.shape, lambda s, *_: (0, 0)) for v in lefts]
            + [spec(i) for _ in range(factors) for i in range(parts)],
            out_specs=pl.BlockSpec(
                (count, block), lambda s, p: (0, p[s // steps] // block + s % steps)
            ),
        ),
        out_shape=jax.ShapeDtypeStruct((count, parts * size), jnp.bfloat16),
        compiler_params=pltpu.CompilerParams(vmem_limit_bytes=60 * MIB),
        cost_estimate=cost(3 * len(lefts)),
    )(places, *lefts, *[w for weight in weights for w in weight])


def collect_kernel(parts, sets, places, *refs):
    rows, pieces, out = refs[:sets], refs[sets:-1], refs[-1]
    at = 0
    for block in rows:
        total = 0.0
        for i in range(parts):
            columns = pl.ds(pl.multiple_of(places[i], TILE), pieces[i].shape[1])
            total = total + dot(pieces[i][...], block[:, columns], 1, 1)
        out[:, at : at + block.shape[0]] = total.astype(out.dtype)
        at += block.shape[0]


def collect(places, rows, pieces):
    parts, count = len(pieces), sum(v.shape[0] for v in rows)
    units = pieces[0].shape[0]
    block = 256
    specs = [pl.BlockSpec((block, w.shape[1]), lambda i, *_: (i, 0)) for w in pieces]
    return pl.pallas_call(
        functools.partial(collect_kernel, parts, len(rows)),
        grid_spec=pltpu.PrefetchScalarGridSpec(
            num_scalar_prefetch=1,
            grid=(units // block,),
            in_specs=[pl.BlockSpec(v.shape, lambda i, *_: (0, 0)) for v in rows] + specs,
            out_specs=pl.BlockSpec((block, count), lambda i, *_: (i, 0)),
        ),
        out_shape=jax.ShapeDtypeStruct((units, count), jnp.bfloat16),
        compiler_params=pltpu.CompilerParams(vmem_limit_bytes=60 * MIB),
        cost_estimate=cost(5),
    )(places, *rows, *pieces)


def weigh_kernel(parts, at_left, at_right, wide, places, *refs):
    lefts, rights, out = refs[:parts], refs[parts:-1], refs[-1]
    columns = pl.ds(pl.multiple_of(places[at_right], TILE), wide)
    total = 0.0
    for left, right in zip(lefts, rights):
        total = total + dot(left[...], right[:, columns], 0, 0)
    out[...] = total.astype(out.dtype)


def weigh(places, lefts, at_left, tall, rights, at_right, wide):
    parts = len(lefts)
    count = lefts[0].shape[0]
    block = TILE if tall % 256 or lefts[0].shape[1] % 256 else 256
    return pl.pallas_call(
        functools.partial(weigh_kernel, parts, at_left, at_right, wide),
        grid_spec=pltpu.PrefetchScalarGridSpec(
            num_scalar_prefetch=1,
            grid=(tall // block,),
            in_specs=[
                pl.BlockSpec((count, block), lambda i, p: (0, p[at_left] // block + i))
                for _ in lefts
            ]
            + [pl.BlockSpec(v.shape, lambda i, p: (0, 0)) for v in rights],
            out_specs=pl.BlockSpec((block, wide), lambda i, p: (i, 0)),
        ),
        out_shape=jax.ShapeDtypeStruct((tall, wide), jnp.bfloat16),
        compiler_params=pltpu.CompilerParams(vmem_limit_bytes=60 * MIB),
        cost_estimate=cost(6),
    )(places, *lefts, *rights)


def plus_kernel(left, right, out):
    out[...] = (left[...].astype(jnp.float32) + right[...].astype(jnp.float32)).astype(out.dtype)


def plus(left, right):
    rows, width = left.shape
    block = rows // 4 if rows % 64 == 0 else rows
    spec = pl.BlockSpec((block, width), lambda i: (i, 0))
    return pl.pallas_call(
        plus_kernel,
        grid=(rows // block,),
        in_specs=[spec, spec],
        out_specs=spec,
        out_shape=jax.ShapeDtypeStruct(left.shape, left.dtype),
        compiler_params=pltpu.CompilerParams(vmem_limit_bytes=60 * MIB),
        cost_estimate=SMALL,
    )(left, right)


def entry_kernel(parts, query_steps, places, rows, cosine, sine, *refs):
    pieces, (q, kv) = refs[:parts], refs[parts:]
    step = pl.program_id(0)
    total = 0.0
    for i in range(parts):
        columns = pl.ds(pl.multiple_of(places[i], TILE), pieces[i].shape[0])
        total = total + dot(pieces[i][...], rows[:, columns], 0, 1)
    half = HD // 2

    def turned(start):
        former, latter = total[start : start + half], total[start + half : start + HD]
        return jnp.concatenate(
            [
                former * cosine[...] - latter * sine[...],
                latter * cosine[...] + former * sine[...],
            ],
            axis=0,
        ).astype(jnp.bfloat16)

    @pl.when(step < query_steps)
    def _():
        for start in (0, HD):
            q[start : start + HD] = turned(start) * 0.125

    @pl.when(step == query_steps)
    def _():
        keys = turned(0)
        values = total[HD:].astype(jnp.bfloat16)
        for j in range(kv.shape[0]):
            columns = slice(j * TILE, (j + 1) * TILE)
            kv[j, :HD] = keys[:, columns]
            kv[j, HD:] = values[:, columns]


def entry(places, rows, cosine, sine, pieces):
    parts = len(pieces)
    count, width = rows.shape
    steps = pieces[0].shape[1] // TILE - 1
    table = pl.BlockSpec(cosine.shape, lambda i, *_: (0, 0))
    return pl.pallas_call(
        functools.partial(entry_kernel, parts, steps),
        grid_spec=pltpu.PrefetchScalarGridSpec(
            num_scalar_prefetch=1,
            grid=(steps + 1,),
            in_specs=[pl.BlockSpec((count, width), lambda i, *_: (0, 0)), table, table]
            + [pl.BlockSpec((w.shape[0], TILE), lambda i, *_: (0, i)) for w in pieces],
            out_specs=[
                pl.BlockSpec((TILE, count), lambda i, *_: (jnp.minimum(i, steps - 1), 0)),
                pl.BlockSpec((count // TILE, TILE, TILE), lambda i, *_: (0, 0, 0)),
            ],
        ),
        out_shape=[
            jax.ShapeDtypeStruct((steps * TILE, count), jnp.bfloat16),
            jax.ShapeDtypeStruct((count // TILE, TILE, TILE), jnp.bfloat16),
        ],
        compiler_params=pltpu.CompilerParams(vmem_limit_bytes=60 * MIB),
        cost_estimate=SMALL,
    )(places, rows, cosine, sine, *pieces)


def place_kernel(order, first, second, out):
    step = pl.program_id(0)

    @pl.when(step < 2)
    def _():
        out[...] = first[...].astype(out.dtype)

    @pl.when(step >= 2)
    def _():
        out[...] = second[...].astype(out.dtype)


def place(order, halves, dtype):
    size, width = halves[0].shape[0] // 2, halves[0].shape[1]
    return pl.pallas_call(
        place_kernel,
        grid_spec=pltpu.PrefetchScalarGridSpec(
            num_scalar_prefetch=1,
            grid=(4,),
            in_specs=[
                pl.BlockSpec((size, width), lambda i, *_: (jnp.minimum(i, 1), 0)),
                pl.BlockSpec((size, width), lambda i, *_: (jnp.maximum(i - 2, 0), 0)),
            ],
            out_specs=pl.BlockSpec((size, width), lambda i, o: (o[i], 0)),
        ),
        out_shape=jax.ShapeDtypeStruct((4 * size, width), dtype),
        compiler_params=pltpu.CompilerParams(vmem_limit_bytes=60 * MIB),
        cost_estimate=cost(5),
    )(order, *halves)


def finish_kernel(axis, where, *refs):
    pieces, out = refs[:-1], refs[-1]
    for i in range(len(pieces) // 2):
        total = jnp.where(where[0] != 0, pieces[2 * i][...], pieces[2 * i + 1][...])
        total = total.astype(jnp.float32)
        at = pl.ds(pl.multiple_of(where[1 + i], TILE), total.shape[axis])
        if len(pieces) == 2:
            out[...] = total
        elif axis == 0:
            out[at] = total
        else:
            out[:, at] = total


def finish(where, axis, kept, *came):
    shape = list(kept.shape)
    shape[axis] += came[1].shape[axis] if len(came) > 1 else 0
    block = 256 if shape[1 - axis] % 256 == 0 else shape[1 - axis]

    def spec(size):
        if axis == 0:
            return pl.BlockSpec((size, block), lambda s, *_: (0, s))
        return pl.BlockSpec((block, size), lambda s, *_: (s, 0))

    return pl.pallas_call(
        functools.partial(finish_kernel, axis),
        grid_spec=pltpu.PrefetchScalarGridSpec(
            num_scalar_prefetch=1,
            grid=(shape[1 - axis] // block,),
            in_specs=[spec(p.shape[axis]) for p in (kept, *came)],
            out_specs=spec(shape[axis]),
        ),
        out_shape=jax.ShapeDtypeStruct(shape, jnp.float32),
        compiler_params=pltpu.CompilerParams(vmem_limit_bytes=60 * MIB),
        cost_estimate=cost(6),
    )(where, kept, *came)


def rms_scale(values):
    return lax.rsqrt(jnp.mean(values * values, axis=-1, keepdims=True) + epsilon)


def norm_back(values, scale, gain, upstream):
    weighted = upstream * gain
    return scale * weighted - values * scale**3 * jnp.mean(
        values * weighted, axis=-1, keepdims=True
    )


def turn(values, cosine, sine):
    half = HD // 2
    former, latter = values[:, :half], values[:, half:]
    return jnp.concatenate(
        [former * cosine - latter * sine, latter * cosine + former * sine], axis=1
    )


def per_device(
    sizes,
    tokens,
    first_gain,
    query_weight,
    keyval_weight,
    output_weight,
    second_gain,
    gate_weight,
    up_weight,
    down_weight,
    segment_ids,
    positions,
    cotangent,
):
    nx, nz, nt = sizes
    low, high = jnp.bfloat16, jnp.float32
    rows, width = tokens.shape
    block = rows // nt
    half = width // nx
    here_x, here_z, here_t = (lax.axis_index(a) for a in ("fsdp", "ctx", "tp"))
    paired = nx == 2
    assert nt == 4 and block % TILE == 0 and keyval_weight.shape[1] == 2 * HD
    order = jnp.stack([here_t ^ k for k in ORDER]).astype(jnp.int32)

    def arranged(whole, axis=0):
        return jnp.concatenate(
            [
                lax.dynamic_slice_in_dim(whole, (here_t ^ k) * block, block, axis)
                for k in ORDER
            ],
            axis=axis,
        )

    def part(whole, start, size, axis):
        return lax.dynamic_slice_in_dim(whole, start, size, axis)

    def mine(whole):
        return part(whole, here_x * half, half, 1)

    def theirs(whole):
        return part(whole, (1 - here_x) * half, half, 1)

    units = gate_weight.shape[1]
    query_width = query_weight.shape[1]
    heads = query_width // HD
    qkv_shard = jnp.concatenate([query_weight, keyval_weight], axis=1)
    gain_shards = jnp.stack([first_gain, second_gain])
    if paired:
        big = (units // TILE + 1) // 2 * TILE
        small = units - big
        spare = big - small
        places = jnp.stack(
            [here_x * half, (1 - here_x) * half, here_x, 0 * here_x, here_x * spare]
        ).astype(jnp.int32)
        at, at_theirs = here_x * small, (1 - here_x) * small
        gains_there = over_x(gain_shards)
        gains = jnp.where(
            here_x == 0,
            jnp.concatenate([gain_shards, gains_there], axis=1),
            jnp.concatenate([gains_there, gain_shards], axis=1),
        )
        qkv_w = (qkv_shard, over_x(qkv_shard))
        output_w = (output_weight, over_x(output_weight))
        fourth = half // nz

        def around(received):
            return lax.all_gather(received, "ctx", axis=0, tiled=True)

        def columns(weight):
            start = (here_z * fourth, at_theirs)
            return over_x(lax.dynamic_slice(weight, start, (fourth, big)))

        gate_fourth, upper_fourth = columns(gate_weight), columns(up_weight)
        gate_own, upper_own = part(gate_weight, at, big, 1), part(up_weight, at, big, 1)
        down_w = (part(down_weight, at, big, 0), over_x(part(down_weight, at_theirs, big, 0)))
    else:
        spare = 0
        places = jnp.zeros((2,), jnp.int32)
        whole = lambda shard, dim: lax.all_gather(shard, "fsdp", axis=dim, tiled=True)
        gains = whole(gain_shards, 1)
        qkv_w, output_w = (whole(qkv_shard, 0),), (whole(output_weight, 1),)
        gate_w, upper_w = (whole(gate_weight, 0),), (whole(up_weight, 0),)
        down_w = (whole(down_weight, 1),)
    gains = gains.astype(high)
    gain_one, gain_two = gains[0], gains[1]

    codes = arranged((segment_ids * CODE + positions).reshape(nz, rows), 1)
    bases = arranged((segment_ids * CODE).reshape(nz, rows), 1)
    q_code = lax.dynamic_index_in_dim(codes, here_z, 0, False)
    q_base = lax.dynamic_index_in_dim(bases, here_z, 0, False)
    k_code = jnp.concatenate(
        [
            lax.dynamic_index_in_dim(codes, (here_z + nz - d) % nz, 0, False)
            for d in range(nz)
        ]
    )
    count, tiles = plan_tiles(q_code, q_base, k_code)
    k_wide = jnp.broadcast_to(k_code.reshape(-1, TILE, 1), (nz * rows // TILE, TILE, TILE))
    masks = (q_code[None], q_base[None], k_wide)
    spots = (q_code - q_base).astype(high)
    freqs = jnp.exp(jnp.arange(HD // 2).astype(high) * (-2.0 * math.log(10000.0) / HD))
    angles = freqs[:, None] * spots[None, :]
    cosine, sine = jnp.cos(angles), jnp.sin(angles)

    tokens = arranged(tokens)
    cotangent = arranged(cotangent)
    inputs = tokens.astype(high)
    scale_one = rms_scale(inputs)
    normed_one = (inputs * scale_one * gain_one).astype(low)
    q, kv = entry(places, normed_one, cosine, sine, qkv_w)
    q = q.reshape(heads, HD, rows)
    kv = jnp.concatenate([kv] + [shift(kv, "ctx", nz, d) for d in range(1, nz)], axis=0)
    if paired:
        gate_fourth, upper_fourth = after([gate_fourth, upper_fourth], kv)
        gate_w = (gate_own, around(gate_fourth))
        upper_w = (upper_own, around(upper_fourth))

    mixed, lse = attend(count, tiles, q, kv, *masks)
    mixed_low = mixed.reshape(query_width, rows).astype(low)
    attn = project(places, [mixed_low], [output_w], 0, 0)
    keep, give = cut(attn[None], 1)
    attn_own, _ = scatter_rows(keep, give)
    one_own = inputs[:block] + attn_own
    scale_two = rms_scale(one_own)
    normed_own = (one_own * scale_two * gain_two).astype(low)

    if paired:
        there = over_x(cotangent[:block])
        there = jnp.concatenate([there, over_y(there)], axis=0)
        upstream = [
            jnp.concatenate([c, t], axis=0)
            for c, t in zip(jnp.split(cotangent, 2), (there, over_core(there)))
        ]
        (normed_own,) = after([normed_own], *upstream, down_w[1], gate_w[1])
        normed_two = gather_pair(normed_own, upper_w[1])
    else:
        normed_two = gather_own(normed_own)
        upstream = jnp.split(cotangent, 2)
    normed_two = [v.reshape(-1, width) for v in normed_two]
    sets = 2 if paired else 1

    def spread(value, dim):
        return lax.psum_scatter(value, "fsdp", scatter_dimension=dim, tiled=True)

    grads = [outer(places, u, down_w) for u in upstream]

    def forward(i):
        return middle(places, normed_two[i], grads[i], gate_w, upper_w)

    def back(i):
        made = project(places, [dgate[i], dupper[i]], [gate_w, upper_w], 1, 1, spare)
        return made.reshape(sets, -1, width)

    def ffn(i):
        return project(places, [hidden[i]], [down_w], 1, 0, spare).reshape(sets, -1, width)

    line = Line()
    hidden, dgate, dupper = [None, None], [None, None], [None, None]
    if paired:
        mixed_there, one_there = after([mixed_low, theirs(normed_one)], grads[0])
        mixed_there, one_there = over_x(mixed_there), over_x(one_there)
    for i in range(2):
        hidden[i], dgate[i], dupper[i] = forward(i)
    if paired:
        line.put(weigh(places, hidden, 3, big, upstream, 0, half))
        line.put(weigh(places, normed_two, 0, half, dgate, 3, big))
        line.put(weigh(places, normed_two, 0, half, dupper, 3, big))
    else:
        weight_grad = lambda lefts, rights: sum(
            dot(left, right, 0, 0) for left, right in zip(lefts, rights)
        ).astype(low)
        line.put(spread(weight_grad(hidden, upstream), 1))
        line.put(spread(weight_grad(normed_two, dgate), 0))
        line.put(spread(weight_grad(normed_two, dupper), 0))
    given = back(1)
    if paired:
        (places,) = after([places], given, mixed_there, one_there)
    grad_own, sent = scatter_rows(back(0), given)
    grad_one = cotangent[:block].astype(high) + norm_back(
        one_own, scale_two, gain_two, grad_own
    )
    grad_one_low = grad_one.astype(low)
    gain_two_sum = jnp.sum(grad_own * one_own * scale_two, axis=0)
    grad_attn = gather_own(grad_one_low)
    if paired:
        given = weigh(places, hidden, 4, small, upstream, 1, half)
        (given,) = after([given], *sent)
        came_down = over_x(given)
        line.put(came_down)
        given = weigh(places, normed_two, 1, half, dgate, 4, small)
        (given,) = after([given], came_down)
        came_gate = over_x(given)
        line.put(came_gate)
        given = weigh(places, normed_two, 1, half, dupper, 4, small)
        (given,) = after([given], came_gate)
        came_upper = over_x(given)
        line.put(came_upper)
    grad_mixed = collect(places, grad_attn, output_w).reshape(heads, HD, rows)
    grad_attn = jnp.concatenate(grad_attn, axis=0)

    dq, dkv = attend_back(count, tiles, q, kv, *masks, mixed, lse, grad_mixed)
    per = rows // TILE
    dkv_own = dkv[:per]
    moved = [dkv[d * per : (d + 1) * per].astype(low) for d in range(1, nz)]
    received = [shift(m, "ctx", nz, nz - 1 - d) for d, m in enumerate(moved)]
    if paired:
        (attn_there,) = after([theirs(grad_attn)], came_upper)
        output_grad = dot(mixed_low, mine(grad_attn), 1, 0) + dot(
            mixed_there, over_x(attn_there), 1, 0
        )
        line.put(output_grad.astype(low))
    else:
        line.put(spread(dot(mixed_low, grad_attn, 1, 0).astype(low), 1))
    for m in received:
        dkv_own = dkv_own + m.astype(high)
    dkv_own = jnp.transpose(dkv_own, (1, 0, 2)).reshape(2 * HD, rows)
    dq = turn(dq * 0.125, cosine, -sine).reshape(query_width, rows)
    dk = turn(dkv_own[None, :HD], cosine, -sine)[0]
    dqkv = jnp.concatenate([dq, dk, dkv_own[HD:]], axis=0).astype(low)
    first = project(places, [dqkv], [qkv_w], 0, 1)
    keep, give = cut(first[None], 1)
    first_own, _ = scatter_rows(keep, give)
    if paired:
        qkv_grad = (
            dot(mine(normed_one), dqkv, 0, 1) + dot(one_there, over_x(dqkv), 0, 1)
        ).astype(low)
    else:
        qkv_grad = spread(dot(normed_one, dqkv, 0, 1).astype(low), 0)
    scale_own = scale_one[:block]
    inputs_own = inputs[:block]
    gain_one_sum = jnp.sum(first_own * inputs_own * scale_own, axis=0)
    input_own = grad_one + norm_back(inputs_own, scale_own, gain_one, first_own)
    input_grad = place(order, gather_own(input_own.astype(low)), high)
    ffn_own, _ = scatter_rows(ffn(0), ffn(1))
    activations = place(order, gather_own((one_own + ffn_own).astype(low)), low)

    gain_sums = sum_all(jnp.stack([gain_one_sum, gain_two_sum]), "tp", nt)
    if paired:
        gain_sums = mine(gain_sums) + over_x(theirs(gain_sums))
    else:
        gain_sums = lax.psum_scatter(gain_sums, "fsdp", scatter_dimension=1, tiled=True)
    upper_half, lower_half = jnp.split(qkv_grad, 2)
    line.put(upper_half)
    long = lower_half.shape[1]
    extra = -(-gain_sums.size // (16 * long)) * 16
    gain_sums = jnp.pad(gain_sums.reshape(-1), (0, extra * long - gain_sums.size))
    gain_sums = gain_sums.reshape(extra, long).astype(low)
    line.put(jnp.concatenate([lower_half, gain_sums], axis=0))
    assert nz == 4
    inner = ((here_z == 1) | (here_z == 2)).astype(jnp.int32)
    if paired:
        where = jnp.stack([inner, here_x * small, (1 - here_x) * big]).astype(jnp.int32)
    else:
        where = jnp.stack([inner, 0, 0]).astype(jnp.int32)
    def whole(i):
        return jnp.where(inner != 0, line.total[i], line.done[i])

    down_grad, gate_grad, upper_grad = (
        finish(where, axis, *(v for k in ((i, i + 3) if paired else (i,)) for v in (line.total[k], line.done[k])))
        for i, axis in ((0, 0), (1, 1), (2, 1))
    )
    output_grad = whole(-3).astype(high)
    qkv_grad = jnp.concatenate([whole(-2), whole(-1)[:-extra]], axis=0).astype(high)
    gain_sums = whole(-1)[-extra:].astype(high).reshape(-1)[: 2 * half].reshape(2, half)
    return (
        activations,
        input_grad,
        gain_sums[0],
        qkv_grad[:, :query_width],
        qkv_grad[:, query_width:],
        output_grad,
        gain_sums[1],
        gate_grad,
        upper_grad,
        down_grad,
    )


def solution(mesh):
    placed = (
        P(("fsdp", "ctx"), None),
        P("fsdp"),
        P("fsdp", "tp"),
        P("fsdp", "tp"),
        P("tp", "fsdp"),
        P("fsdp"),
        P("fsdp", "tp"),
        P("fsdp", "tp"),
        P("tp", "fsdp"),
        P("fsdp"),
        P("fsdp"),
        P(("fsdp", "ctx"), None),
    )
    sizes = (mesh.shape["fsdp"], mesh.shape["ctx"], mesh.shape["tp"])
    return jax.shard_map(
        functools.partial(per_device, sizes),
        mesh=mesh,
        in_specs=placed,
        out_specs=(
            P(("fsdp", "ctx"), None),
            P(("fsdp", "ctx"), None),
            P("fsdp"),
            P("fsdp", "tp"),
            P("fsdp", "tp"),
            P("tp", "fsdp"),
            P("fsdp"),
            P("fsdp", "tp"),
            P("fsdp", "tp"),
            P("tp", "fsdp"),
        ),
        check_vma=False,
    )
```

```python
import functools
import math

import jax
import jax.numpy as jnp
from jax import lax
from jax.experimental import pallas as pl
from jax.experimental.pallas import tpu as pltpu
from jax.sharding import PartitionSpec as P

HD = 64
TILE = 128
CODE = 4096
NEGATIVE = -1e30
epsilon = 1e-05
MIB = 2**20
SMALL = pl.CostEstimate(flops=1000000, bytes_accessed=100000, transcendentals=0)


def cost(microseconds):
    return pl.CostEstimate(
        flops=1000000, bytes_accessed=int(microseconds * SCALE * 3.69e6), transcendentals=0
    )


SCALE = 0.5


def dot(left, right, over_left, over_right):
    return lax.dot_general(
        left,
        right,
        (((over_left,), (over_right,)), ((), ())),
        preferred_element_type=jnp.float32,
    )


ORDER = (0, 2, 1, 3)


def swap(value, axis, distance, size):
    pairs = [(i, i ^ distance) for i in range(size)]
    return lax.ppermute(value, axis, pairs)


def shift(value, axis, size, distance):
    pairs = [(i, (i + distance) % size) for i in range(size)]
    return lax.ppermute(value, axis, pairs)


def over_x(value):
    return swap(value, "fsdp", 1, 2)


def over_y(value):
    return swap(value, "tp", 2, 4)


def over_core(value):
    return swap(value, "tp", 1, 4)


def add(left, right):
    return left.astype(jnp.float32) + right.astype(jnp.float32)


def cut(value, axis=0):
    keep, give = jnp.split(value, 2, axis=axis)
    return keep, give.astype(jnp.bfloat16)


def scatter_rows(keep, give, between=None):
    part = add(keep, over_core(give)).astype(jnp.bfloat16)
    if part.shape[0] == 1:
        keep, give = cut(part[0])
        return add(keep, over_y(give)), [give]
    left, right = jnp.split(part, 2, axis=2)
    keep_left, give_left = cut(left)
    keep_right, give_right = cut(right, 1)
    from_x, from_y = over_x(give_left), over_y(give_right)
    if between:
        from_x, from_y = after([from_x, from_y], *between([give_left, give_right]))
    left = add(keep_left, from_x)[0]
    right = add(keep_right, from_y)
    keep_left, give_left = cut(left)
    keep_right, give_right = cut(right)
    left = add(keep_left, over_y(give_left))
    right = add(keep_right, over_x(give_right))[0]
    return jnp.concatenate([left, right], axis=1), [give_left, give_right]


def both_cores(rows):
    first = over_x(rows[: rows.shape[0] // 2])
    return jnp.concatenate([first, over_core(first)], axis=0)


def gather_own(rows, *tokens):
    first = jnp.concatenate([rows, over_y(rows)], axis=0)
    if tokens:
        (first,) = after([first], *tokens)
    return first, over_core(first)


def gather_pair(rows, early=(), late=()):
    left, right = jnp.split(rows, 2, axis=1)
    left = jnp.stack([left, over_x(left)])
    right = jnp.concatenate([right, over_y(right)], axis=0)
    if early:
        left, right = after([left, right], *early)
    left = jnp.concatenate([left, over_y(left)], axis=1)
    right = jnp.stack([right, over_x(right)])
    first = jnp.concatenate([left, right], axis=2)
    if late:
        (first,) = after([first], *late)
    return first, over_core(first)


def sum_all(value, axis, size):
    distance = 1
    while distance < size:
        value = value + swap(value, axis, distance, size)
        distance *= 2
    return value


class Line:
    def __init__(self):
        self.piece, self.came, self.total, self.done = [], [], [], []

    def put(self, piece):
        k = len(self.came)
        far = k - 1
        earlier = [v[i] for v, i in ((self.came, far), (self.total, far - 1), (self.done, far - 2)) if i >= 0]
        if earlier:
            (piece,) = after([piece], *earlier)
        self.piece.append(piece)
        self.came.append(lax.ppermute(piece, "ctx", [(0, 1), (3, 2)]))
        inward = piece + self.came[-1]
        self.total.append(inward + lax.ppermute(inward, "ctx", [(1, 2), (2, 1)]))
        self.done.append(lax.ppermute(self.total[-1], "ctx", [(1, 0), (2, 3)]))
        return len(self.total) - 1


def attend_kernel(
    heads, count, tiles, q, kv, q_code, q_base, k_code, mixed, lse, top, total, acc
):
    step = pl.program_id(0)
    top[...] = jnp.full_like(top, NEGATIVE)
    total[...] = jnp.zeros_like(total)
    acc[...] = jnp.zeros_like(acc)
    code, base = q_code[...], q_base[...]

    def body(j, carry):
        tile = tiles[step, j]
        keys = kv[tile, :HD]
        values = kv[tile, HD:]
        key_code = k_code[tile]
        allowed = (key_code <= code) & (key_code >= base)
        for h in range(heads):
            scores = jnp.where(allowed, dot(keys, q[h], 0, 0), NEGATIVE)
            before = top[h : h + 1]
            highest = jnp.maximum(before, jnp.max(scores, axis=0, keepdims=True))
            probs = jnp.exp(scores - highest)
            fade = jnp.exp(before - highest)
            top[h : h + 1] = highest
            total[h : h + 1] = total[h : h + 1] * fade + jnp.sum(probs, axis=0, keepdims=True)
            acc[h] = acc[h] * fade + dot(values, probs.astype(jnp.bfloat16), 1, 0)
        return carry

    lax.fori_loop(0, count[step], body, 0)
    sums = total[...]
    lse[...] = top[...] + jnp.log(sums)
    inverse = 1.0 / sums
    for h in range(heads):
        mixed[h] = acc[h] * inverse[h : h + 1]


def attend(count, tiles, q, kv, q_code, q_base, k_code):
    heads, _, rows = q.shape
    stack = pl.BlockSpec(kv.shape, lambda i, *_: (0, 0, 0))
    codes = pl.BlockSpec(k_code.shape, lambda i, *_: (0, 0, 0))
    line = pl.BlockSpec((1, TILE), lambda i, *_: (0, i))
    block = pl.BlockSpec((heads, HD, TILE), lambda i, *_: (0, 0, i))
    return pl.pallas_call(
        functools.partial(attend_kernel, heads),
        grid_spec=pltpu.PrefetchScalarGridSpec(
            num_scalar_prefetch=2,
            grid=(rows // TILE,),
            in_specs=[block, stack, line, line, codes],
            out_specs=[block, pl.BlockSpec((heads, TILE), lambda i, *_: (0, i))],
            scratch_shapes=[
                pltpu.VMEM((heads, TILE), jnp.float32),
                pltpu.VMEM((heads, TILE), jnp.float32),
                pltpu.VMEM((heads, HD, TILE), jnp.float32),
            ],
        ),
        out_shape=[
            jax.ShapeDtypeStruct((heads, HD, rows), jnp.float32),
            jax.ShapeDtypeStruct((heads, rows), jnp.float32),
        ],
        compiler_params=pltpu.CompilerParams(vmem_limit_bytes=60 * MIB),
        cost_estimate=SMALL,
    )(count, tiles, q, kv, q_code, q_base, k_code)


def attend_back_kernel(
    heads, count, tiles, q, kv, q_code, q_base, k_code, mixed, lse, upstream, dq, dkv, centre
):
    step = pl.program_id(0)

    @pl.when(step == 0)
    def _():
        dkv[...] = jnp.zeros_like(dkv)

    dq[...] = jnp.zeros_like(dq)
    code, base = q_code[...], q_base[...]
    for h in range(heads):
        centre[h : h + 1] = jnp.sum(
            mixed[h] * upstream[h].astype(jnp.float32), axis=0, keepdims=True
        )

    def body(j, carry):
        tile = tiles[step, j]
        keys = kv[tile, :HD]
        values = kv[tile, HD:]
        key_code = k_code[tile]
        allowed = (key_code <= code) & (key_code >= base)
        key_term = dkv[tile, :HD]
        value_term = dkv[tile, HD:]
        for h in range(heads):
            scores = dot(keys, q[h], 0, 0) - lse[h : h + 1]
            probs = jnp.exp(jnp.where(allowed, scores, NEGATIVE))
            grad_probs = dot(values, upstream[h], 0, 0)
            grad_scores = (probs * (grad_probs - centre[h : h + 1])).astype(jnp.bfloat16)
            value_term = value_term + dot(upstream[h], probs.astype(jnp.bfloat16), 1, 1)
            key_term = key_term + dot(q[h], grad_scores, 1, 1)
            dq[h] += dot(keys, grad_scores, 1, 0)
        dkv[tile, :HD] = key_term
        dkv[tile, HD:] = value_term
        return carry

    lax.fori_loop(0, count[step], body, 0)


def attend_back(count, tiles, q, kv, q_code, q_base, k_code, mixed, lse, upstream):
    heads, _, rows = q.shape
    stack = pl.BlockSpec(kv.shape, lambda i, *_: (0, 0, 0))
    codes = pl.BlockSpec(k_code.shape, lambda i, *_: (0, 0, 0))
    line = pl.BlockSpec((1, TILE), lambda i, *_: (0, i))
    block = pl.BlockSpec((heads, HD, TILE), lambda i, *_: (0, 0, i))
    return pl.pallas_call(
        functools.partial(attend_back_kernel, heads),
        grid_spec=pltpu.PrefetchScalarGridSpec(
            num_scalar_prefetch=2,
            grid=(rows // TILE,),
            in_specs=[
                block,
                stack,
                line,
                line,
                codes,
                block,
                pl.BlockSpec((heads, TILE), lambda i, *_: (0, i)),
                block,
            ],
            out_specs=[block, stack],
            scratch_shapes=[pltpu.VMEM((heads, TILE), jnp.float32)],
        ),
        out_shape=[
            jax.ShapeDtypeStruct((heads, HD, rows), jnp.float32),
            jax.ShapeDtypeStruct(kv.shape, jnp.float32),
        ],
        compiler_params=pltpu.CompilerParams(vmem_limit_bytes=60 * MIB),
        cost_estimate=cost(24),
    )(count, tiles, q, kv, q_code, q_base, k_code, mixed, lse, upstream)


def plan_tiles(q_code, q_base, k_code):
    rows, keys = q_code.shape[0], k_code.shape[0]
    allowed = (k_code[None, :] <= q_code[:, None]) & (k_code[None, :] >= q_base[:, None])
    used = jnp.any(allowed.reshape(rows // TILE, TILE, keys // TILE, TILE), axis=(1, 3))
    place = jnp.cumsum(used.astype(jnp.int32), axis=1) - 1
    ladder = jnp.arange(keys // TILE)
    hit = used[:, :, None] & (place[:, :, None] == ladder[None, None, :])
    tiles = jnp.sum(jnp.where(hit, ladder[None, :, None], 0), axis=1).astype(jnp.int32)
    return jnp.sum(used.astype(jnp.int32), axis=1), tiles


def nothing(*refs):
    pass


def after(values, *tokens):
    anywhere = pl.BlockSpec(memory_space=pl.ANY)
    return pl.pallas_call(
        nothing,
        in_specs=[anywhere] * (len(values) + len(tokens)),
        out_specs=[anywhere] * len(values),
        out_shape=[jax.ShapeDtypeStruct(v.shape, v.dtype) for v in values],
        input_output_aliases={i: i for i in range(len(values))},
    )(*values, *tokens)


def outer_kernel(parts, places, upstream, *refs):
    pieces, out = refs[:parts], refs[parts]
    total = 0.0
    for i in range(parts):
        columns = pl.ds(pl.multiple_of(places[i], TILE), pieces[i].shape[1])
        total = total + dot(upstream[:, columns], pieces[i][...], 1, 1)
    out[...] = total


def outer(places, upstream, down_w):
    count, width = upstream.shape
    units = down_w[0].shape[0]
    block = 256
    flat = [pl.BlockSpec((block, w.shape[1]), lambda i, *_: (i, 0)) for w in down_w]
    return pl.pallas_call(
        functools.partial(outer_kernel, len(down_w)),
        grid_spec=pltpu.PrefetchScalarGridSpec(
            num_scalar_prefetch=1,
            grid=(pl.cdiv(units, block),),
            in_specs=[pl.BlockSpec((count, width), lambda i, *_: (0, 0)), *flat],
            out_specs=pl.BlockSpec((count, block), lambda i, *_: (0, i)),
        ),
        out_shape=jax.ShapeDtypeStruct((count, units), jnp.float32),
        compiler_params=pltpu.CompilerParams(vmem_limit_bytes=60 * MIB),
        cost_estimate=SMALL,
    )(places, upstream, *down_w)


def middle_kernel(parts, places, rows, grads, *refs):
    pieces, (hidden, dgate, dupper) = refs[: 2 * parts], refs[2 * parts :]
    gate = upper = 0.0
    for i in range(parts):
        columns = pl.ds(pl.multiple_of(places[i], TILE), pieces[i].shape[0])
        left = rows[:, columns]
        gate = gate + dot(left, pieces[i][...], 1, 0)
        upper = upper + dot(left, pieces[parts + i][...], 1, 0)
    grad = grads[...]
    sigma = 1.0 / (1.0 + jnp.exp(-gate))
    swish = gate * sigma
    hidden[...] = (swish * upper).astype(jnp.bfloat16)
    dgate[...] = (grad * upper * sigma * (1.0 + gate * (1.0 - sigma))).astype(jnp.bfloat16)
    dupper[...] = (grad * swish).astype(jnp.bfloat16)


def middle(places, rows, grads, gate_w, upper_w):
    parts = len(gate_w)
    count, width = rows.shape
    units = gate_w[0].shape[1]
    block = 256
    out = pl.BlockSpec((count, block), lambda i, *_: (0, i))
    tall = [pl.BlockSpec((w.shape[0], block), lambda i, *_: (0, i)) for w in gate_w]
    return pl.pallas_call(
        functools.partial(middle_kernel, parts),
        grid_spec=pltpu.PrefetchScalarGridSpec(
            num_scalar_prefetch=1,
            grid=(pl.cdiv(units, block),),
            in_specs=[pl.BlockSpec((count, width), lambda i, *_: (0, 0)), out, *tall, *tall],
            out_specs=[out, out, out],
        ),
        out_shape=[jax.ShapeDtypeStruct((count, units), jnp.bfloat16)] * 3,
        compiler_params=pltpu.CompilerParams(vmem_limit_bytes=60 * MIB),
        cost_estimate=cost(9),
    )(places, rows, grads, *gate_w, *upper_w)


def project_kernel(parts, factors, steps, over_left, over_right, skip, places, *refs):
    lefts, pieces, out = refs[:factors], refs[factors:-1], refs[-1]
    step = pl.program_id(0)

    def one(i, start):
        total = 0.0
        for f in range(factors):
            left, right = lefts[f], pieces[f * parts + i]
            left = left[:, start:] if over_left else left[start:]
            right = right[:, start:] if over_right else right[start:]
            total = total + dot(left, right, over_left, over_right)
        out[...] = total.astype(out.dtype)

    for i in range(parts):
        here = (step >= i * steps) & (step < (i + 1) * steps)
        if skip:
            pl.when(here & (places[parts] == 0))(functools.partial(one, i, 0))
            pl.when(here & (places[parts] != 0))(functools.partial(one, i, skip))
        else:
            pl.when(here)(functools.partial(one, i, 0))


def project(places, lefts, weights, over_left, over_right, skip=0):
    parts, factors = len(weights[0]), len(lefts)
    axis = 1 - over_right
    size = weights[0][0].shape[axis]
    block = min(512, size)
    steps = size // block
    depth = weights[0][0].shape[over_right]
    count = lefts[0].shape[1 - over_left]

    def spec(i):
        at = lambda s: jnp.clip(s - i * steps, 0, steps - 1)
        if axis == 0:
            return pl.BlockSpec((block, depth), lambda s, *_: (at(s), 0))
        return pl.BlockSpec((depth, block), lambda s, *_: (0, at(s)))

    return pl.pallas_call(
        functools.partial(
            project_kernel, parts, factors, steps, over_left, over_right, skip
        ),
        grid_spec=pltpu.PrefetchScalarGridSpec(
            num_scalar_prefetch=1,
            grid=(parts * steps,),
            in_specs=[pl.BlockSpec(v.shape, lambda s, *_: (0, 0)) for v in lefts]
            + [spec(i) for _ in range(factors) for i in range(parts)],
            out_specs=pl.BlockSpec(
                (count, block), lambda s, p: (0, p[s // steps] // block + s % steps)
            ),
        ),
        out_shape=jax.ShapeDtypeStruct((count, parts * size), jnp.bfloat16),
        compiler_params=pltpu.CompilerParams(vmem_limit_bytes=60 * MIB),
        cost_estimate=cost(3 * len(lefts)),
    )(places, *lefts, *[w for weight in weights for w in weight])


def collect_kernel(parts, sets, places, *refs):
    rows, pieces, out = refs[:sets], refs[sets:-1], refs[-1]
    at = 0
    for block in rows:
        total = 0.0
        for i in range(parts):
            columns = pl.ds(pl.multiple_of(places[i], TILE), pieces[i].shape[1])
            total = total + dot(pieces[i][...], block[:, columns], 1, 1)
        out[:, at : at + block.shape[0]] = total.astype(out.dtype)
        at += block.shape[0]


def collect(places, rows, pieces):
    parts, count = len(pieces), sum(v.shape[0] for v in rows)
    units = pieces[0].shape[0]
    block = 256
    specs = [pl.BlockSpec((block, w.shape[1]), lambda i, *_: (i, 0)) for w in pieces]
    return pl.pallas_call(
        functools.partial(collect_kernel, parts, len(rows)),
        grid_spec=pltpu.PrefetchScalarGridSpec(
            num_scalar_prefetch=1,
            grid=(units // block,),
            in_specs=[pl.BlockSpec(v.shape, lambda i, *_: (0, 0)) for v in rows] + specs,
            out_specs=pl.BlockSpec((block, count), lambda i, *_: (i, 0)),
        ),
        out_shape=jax.ShapeDtypeStruct((units, count), jnp.bfloat16),
        compiler_params=pltpu.CompilerParams(vmem_limit_bytes=60 * MIB),
        cost_estimate=cost(5),
    )(places, *rows, *pieces)


def weigh_kernel(parts, at_left, at_right, wide, places, *refs):
    lefts, rights, out = refs[:parts], refs[parts:-1], refs[-1]
    columns = pl.ds(pl.multiple_of(places[at_right], TILE), wide)
    total = 0.0
    for left, right in zip(lefts, rights):
        total = total + dot(left[...], right[:, columns], 0, 0)
    out[...] = total.astype(out.dtype)


def weigh(places, lefts, at_left, tall, rights, at_right, wide):
    parts = len(lefts)
    count = lefts[0].shape[0]
    block = TILE if tall % 256 or lefts[0].shape[1] % 256 else 256
    return pl.pallas_call(
        functools.partial(weigh_kernel, parts, at_left, at_right, wide),
        grid_spec=pltpu.PrefetchScalarGridSpec(
            num_scalar_prefetch=1,
            grid=(tall // block,),
            in_specs=[
                pl.BlockSpec((count, block), lambda i, p: (0, p[at_left] // block + i))
                for _ in lefts
            ]
            + [pl.BlockSpec(v.shape, lambda i, p: (0, 0)) for v in rights],
            out_specs=pl.BlockSpec((block, wide), lambda i, p: (i, 0)),
        ),
        out_shape=jax.ShapeDtypeStruct((tall, wide), jnp.bfloat16),
        compiler_params=pltpu.CompilerParams(vmem_limit_bytes=60 * MIB),
        cost_estimate=cost(6),
    )(places, *lefts, *rights)


def plus_kernel(left, right, out):
    out[...] = (left[...].astype(jnp.float32) + right[...].astype(jnp.float32)).astype(out.dtype)


def plus(left, right):
    rows, width = left.shape
    block = rows // 4 if rows % 64 == 0 else rows
    spec = pl.BlockSpec((block, width), lambda i: (i, 0))
    return pl.pallas_call(
        plus_kernel,
        grid=(rows // block,),
        in_specs=[spec, spec],
        out_specs=spec,
        out_shape=jax.ShapeDtypeStruct(left.shape, left.dtype),
        compiler_params=pltpu.CompilerParams(vmem_limit_bytes=60 * MIB),
        cost_estimate=SMALL,
    )(left, right)


def entry_kernel(parts, query_steps, places, rows, cosine, sine, *refs):
    pieces, (q, kv) = refs[:parts], refs[parts:]
    step = pl.program_id(0)
    total = 0.0
    for i in range(parts):
        columns = pl.ds(pl.multiple_of(places[i], TILE), pieces[i].shape[0])
        total = total + dot(pieces[i][...], rows[:, columns], 0, 1)
    half = HD // 2

    def turned(start):
        former, latter = total[start : start + half], total[start + half : start + HD]
        return jnp.concatenate(
            [
                former * cosine[...] - latter * sine[...],
                latter * cosine[...] + former * sine[...],
            ],
            axis=0,
        ).astype(jnp.bfloat16)

    @pl.when(step < query_steps)
    def _():
        for start in (0, HD):
            q[start : start + HD] = turned(start) * 0.125

    @pl.when(step == query_steps)
    def _():
        keys = turned(0)
        values = total[HD:].astype(jnp.bfloat16)
        for j in range(kv.shape[0]):
            columns = slice(j * TILE, (j + 1) * TILE)
            kv[j, :HD] = keys[:, columns]
            kv[j, HD:] = values[:, columns]


def entry(places, rows, cosine, sine, pieces):
    parts = len(pieces)
    count, width = rows.shape
    steps = pieces[0].shape[1] // TILE - 1
    table = pl.BlockSpec(cosine.shape, lambda i, *_: (0, 0))
    return pl.pallas_call(
        functools.partial(entry_kernel, parts, steps),
        grid_spec=pltpu.PrefetchScalarGridSpec(
            num_scalar_prefetch=1,
            grid=(steps + 1,),
            in_specs=[pl.BlockSpec((count, width), lambda i, *_: (0, 0)), table, table]
            + [pl.BlockSpec((w.shape[0], TILE), lambda i, *_: (0, i)) for w in pieces],
            out_specs=[
                pl.BlockSpec((TILE, count), lambda i, *_: (jnp.minimum(i, steps - 1), 0)),
                pl.BlockSpec((count // TILE, TILE, TILE), lambda i, *_: (0, 0, 0)),
            ],
        ),
        out_shape=[
            jax.ShapeDtypeStruct((steps * TILE, count), jnp.bfloat16),
            jax.ShapeDtypeStruct((count // TILE, TILE, TILE), jnp.bfloat16),
        ],
        compiler_params=pltpu.CompilerParams(vmem_limit_bytes=60 * MIB),
        cost_estimate=SMALL,
    )(places, rows, cosine, sine, *pieces)


def place_kernel(order, first, second, out):
    step = pl.program_id(0)

    @pl.when(step < 2)
    def _():
        out[...] = first[...].astype(out.dtype)

    @pl.when(step >= 2)
    def _():
        out[...] = second[...].astype(out.dtype)


def place(order, halves, dtype):
    size, width = halves[0].shape[0] // 2, halves[0].shape[1]
    return pl.pallas_call(
        place_kernel,
        grid_spec=pltpu.PrefetchScalarGridSpec(
            num_scalar_prefetch=1,
            grid=(4,),
            in_specs=[
                pl.BlockSpec((size, width), lambda i, *_: (jnp.minimum(i, 1), 0)),
                pl.BlockSpec((size, width), lambda i, *_: (jnp.maximum(i - 2, 0), 0)),
            ],
            out_specs=pl.BlockSpec((size, width), lambda i, o: (o[i], 0)),
        ),
        out_shape=jax.ShapeDtypeStruct((4 * size, width), dtype),
        compiler_params=pltpu.CompilerParams(vmem_limit_bytes=60 * MIB),
        cost_estimate=cost(5),
    )(order, *halves)


def finish_kernel(axis, where, kept, *refs):
    out = refs[-1]
    if len(refs) == 1:
        out[...] = kept[...].astype(jnp.float32)
        return
    came = jnp.where(where[0] != 0, refs[0][...], refs[1][...])
    for i, piece in enumerate((kept[...], came)):
        at = pl.ds(pl.multiple_of(where[1 + i], TILE), piece.shape[axis])
        if axis == 0:
            out[at] = piece.astype(jnp.float32)
        else:
            out[:, at] = piece.astype(jnp.float32)


def finish(where, axis, kept, *came):
    shape = list(kept.shape)
    shape[axis] += came[0].shape[axis] if came else 0
    block = 256 if shape[1 - axis] % 256 == 0 else shape[1 - axis]

    def spec(size):
        if axis == 0:
            return pl.BlockSpec((size, block), lambda s, *_: (0, s))
        return pl.BlockSpec((block, size), lambda s, *_: (s, 0))

    return pl.pallas_call(
        functools.partial(finish_kernel, axis),
        grid_spec=pltpu.PrefetchScalarGridSpec(
            num_scalar_prefetch=1,
            grid=(shape[1 - axis] // block,),
            in_specs=[spec(p.shape[axis]) for p in (kept, *came)],
            out_specs=spec(shape[axis]),
        ),
        out_shape=jax.ShapeDtypeStruct(shape, jnp.float32),
        compiler_params=pltpu.CompilerParams(vmem_limit_bytes=60 * MIB),
        cost_estimate=cost(6),
    )(where, kept, *came)


def rms_scale(values):
    return lax.rsqrt(jnp.mean(values * values, axis=-1, keepdims=True) + epsilon)


def norm_back(values, scale, gain, upstream):
    weighted = upstream * gain
    return scale * weighted - values * scale**3 * jnp.mean(
        values * weighted, axis=-1, keepdims=True
    )


def turn(values, cosine, sine):
    half = HD // 2
    former, latter = values[:, :half], values[:, half:]
    return jnp.concatenate(
        [former * cosine - latter * sine, latter * cosine + former * sine], axis=1
    )


def per_device(
    sizes,
    tokens,
    first_gain,
    query_weight,
    keyval_weight,
    output_weight,
    second_gain,
    gate_weight,
    up_weight,
    down_weight,
    segment_ids,
    positions,
    cotangent,
):
    nx, nz, nt = sizes
    low, high = jnp.bfloat16, jnp.float32
    rows, width = tokens.shape
    block = rows // nt
    half = width // nx
    here_x, here_z, here_t = (lax.axis_index(a) for a in ("fsdp", "ctx", "tp"))
    paired = nx == 2
    assert nt == 4 and block % TILE == 0 and keyval_weight.shape[1] == 2 * HD
    order = jnp.stack([here_t ^ k for k in ORDER]).astype(jnp.int32)

    def arranged(whole, axis=0):
        return jnp.concatenate(
            [
                lax.dynamic_slice_in_dim(whole, (here_t ^ k) * block, block, axis)
                for k in ORDER
            ],
            axis=axis,
        )

    def part(whole, start, size, axis):
        return lax.dynamic_slice_in_dim(whole, start, size, axis)

    def mine(whole):
        return part(whole, here_x * half, half, 1)

    def theirs(whole):
        return part(whole, (1 - here_x) * half, half, 1)

    units = gate_weight.shape[1]
    query_width = query_weight.shape[1]
    heads = query_width // HD
    qkv_shard = jnp.concatenate([query_weight, keyval_weight], axis=1)
    gain_shards = jnp.stack([first_gain, second_gain])
    if paired:
        big = (units // TILE + 1) // 2 * TILE
        small = units - big
        spare = big - small
        places = jnp.stack(
            [here_x * half, (1 - here_x) * half, here_x, 0 * here_x, here_x * spare]
        ).astype(jnp.int32)
        at, at_theirs = here_x * small, (1 - here_x) * small
        gains_there = over_x(gain_shards)
        gains = jnp.where(
            here_x == 0,
            jnp.concatenate([gain_shards, gains_there], axis=1),
            jnp.concatenate([gains_there, gain_shards], axis=1),
        )
        qkv_w = (qkv_shard, over_x(qkv_shard))
        output_w = (output_weight, over_x(after([output_weight], gains_there)[0]))
        fourth = half // nz

        def around(received):
            return lax.all_gather(received, "ctx", axis=0, tiled=True)

        def columns(weight):
            start = (here_z * fourth, at_theirs)
            piece = lax.dynamic_slice(weight, start, (fourth, big))
            return over_x(after([piece], gains_there)[0])

        gate_fourth, upper_fourth = columns(gate_weight), columns(up_weight)
        gate_own, upper_own = part(gate_weight, at, big, 1), part(up_weight, at, big, 1)
        down_w = (part(down_weight, at, big, 0), over_x(part(down_weight, at_theirs, big, 0)))
    else:
        spare = 0
        places = jnp.zeros((2,), jnp.int32)
        whole = lambda shard, dim: lax.all_gather(shard, "fsdp", axis=dim, tiled=True)
        gains = whole(gain_shards, 1)
        qkv_w, output_w = (whole(qkv_shard, 0),), (whole(output_weight, 1),)
        gate_w, upper_w = (whole(gate_weight, 0),), (whole(up_weight, 0),)
        down_w = (whole(down_weight, 1),)
    gains = gains.astype(high)
    gain_one, gain_two = gains[0], gains[1]

    codes = arranged((segment_ids * CODE + positions).reshape(nz, rows), 1)
    bases = arranged((segment_ids * CODE).reshape(nz, rows), 1)
    q_code = lax.dynamic_index_in_dim(codes, here_z, 0, False)
    q_base = lax.dynamic_index_in_dim(bases, here_z, 0, False)
    k_code = jnp.concatenate(
        [
            lax.dynamic_index_in_dim(codes, (here_z + nz - d) % nz, 0, False)
            for d in range(nz)
        ]
    )
    count, tiles = plan_tiles(q_code, q_base, k_code)
    k_wide = jnp.broadcast_to(k_code.reshape(-1, TILE, 1), (nz * rows // TILE, TILE, TILE))
    masks = (q_code[None], q_base[None], k_wide)
    spots = (q_code - q_base).astype(high)
    freqs = jnp.exp(jnp.arange(HD // 2).astype(high) * (-2.0 * math.log(10000.0) / HD))
    angles = freqs[:, None] * spots[None, :]
    cosine, sine = jnp.cos(angles), jnp.sin(angles)

    tokens = arranged(tokens)
    cotangent = arranged(cotangent)
    inputs = tokens.astype(high)
    scale_one = rms_scale(inputs)
    normed_one = (inputs * scale_one * gain_one).astype(low)
    q, kv = entry(places, normed_one, cosine, sine, qkv_w)
    q = q.reshape(heads, HD, rows)
    kv = jnp.concatenate([kv] + [shift(kv, "ctx", nz, d) for d in range(1, nz)], axis=0)
    mixed, lse = attend(count, tiles, q, kv, *masks)
    if paired:
        gate_fourth, upper_fourth = after([gate_fourth, upper_fourth], lse)
        gate_w = (gate_own, around(gate_fourth))
        upper_w = (upper_own, around(upper_fourth))

    mixed_low = mixed.reshape(query_width, rows).astype(low)
    attn = project(places, [mixed_low], [output_w], 0, 0)
    keep, give = cut(attn[None], 1)
    attn_own, _ = scatter_rows(keep, give)
    one_own = inputs[:block] + attn_own
    scale_two = rms_scale(one_own)
    normed_own = (one_own * scale_two * gain_two).astype(low)

    if paired:
        there = over_x(cotangent[:block])
        there = jnp.concatenate([there, over_y(there)], axis=0)
        upstream = [
            jnp.concatenate([c, t], axis=0)
            for c, t in zip(jnp.split(cotangent, 2), (there, over_core(there)))
        ]
        (normed_own,) = after([normed_own], *upstream, down_w[1], gate_w[1])
        grads = [outer(places, u, down_w) for u in upstream]
        normed_two = gather_pair(normed_own, [grads[0]], [grads[1], upper_w[1]])
    else:
        normed_two = gather_own(normed_own)
        upstream = jnp.split(cotangent, 2)
        grads = [outer(places, u, down_w) for u in upstream]
    normed_two = [v.reshape(-1, width) for v in normed_two]
    sets = 2 if paired else 1

    def spread(value, dim):
        return lax.psum_scatter(value, "fsdp", scatter_dimension=dim, tiled=True)

    def forward(i):
        return middle(places, normed_two[i], grads[i], gate_w, upper_w)

    def back(i):
        made = project(places, [dgate[i], dupper[i]], [gate_w, upper_w], 1, 1, spare)
        return made.reshape(sets, -1, width)

    def ffn(i):
        return project(places, [hidden[i]], [down_w], 1, 0, spare).reshape(sets, -1, width)

    line = Line()
    scattered, sums = {}, {}

    def scatter(name, piece):
        scattered[name] = lax.psum_scatter(piece, "ctx", scatter_dimension=0, tiled=True)

    def gather(name, *tokens):
        piece = scattered[name]
        if tokens:
            (piece,) = after([piece], *tokens)
        sums[name] = lax.all_gather(piece, "ctx", axis=0, tiled=True)

    hidden, dgate, dupper = [None, None], [None, None], [None, None]
    if paired:
        hidden[1], dgate[1], dupper[1] = forward(1)
        (places,) = after([places], hidden[1])
        grad_give = back(1)
        (places,) = after([places], grad_give)
        hidden[0], dgate[0], dupper[0] = forward(0)
        (places,) = after([places], hidden[0])
        kept_down = weigh(places, hidden, 3, big, upstream, 0, half)
        scatter("down", kept_down)
        (places,) = after([places], kept_down)
        grad_keep = back(0)
        kept = {}

        def between(sent):
            after_sent = after([places], grad_keep, *sent)[0]
            kept["gate"] = weigh(after_sent, normed_two, 0, half, dgate, 3, big)
            scatter("gate", kept["gate"])
            return [kept["gate"], scattered["down"]]

        grad_own, sent = scatter_rows(grad_keep, grad_give, between)
        (places,) = after([places], kept["gate"], *sent)
        kept_upper = weigh(places, normed_two, 0, half, dupper, 3, big)
        scatter("upper", kept_upper)
        (places,) = after([places], kept_upper)
        (grad_own,) = after([grad_own], kept_upper)
    else:
        for i in range(2):
            hidden[i], dgate[i], dupper[i] = forward(i)
        weight_grad = lambda lefts, rights: sum(
            dot(left, right, 0, 0) for left, right in zip(lefts, rights)
        ).astype(low)
        scatter("down", spread(weight_grad(hidden, upstream), 1))
        scatter("gate", spread(weight_grad(normed_two, dgate), 0))
        scatter("upper", spread(weight_grad(normed_two, dupper), 0))
        grad_own, _ = scatter_rows(back(0), back(1))
    grad_one = cotangent[:block].astype(high) + norm_back(
        one_own, scale_two, gain_two, grad_own
    )
    grad_one_low = grad_one.astype(low)
    gain_two_sum = jnp.sum(grad_own * one_own * scale_two, axis=0)
    grad_attn = gather_own(grad_one_low)
    if paired:
        (places,) = after([places], grad_one_low)
        given_down = weigh(places, hidden, 4, small, upstream, 1, half)
        (places,) = after([places], given_down)
        given_gate = weigh(places, normed_two, 1, half, dgate, 4, small)
        (places,) = after([places], given_gate)
        line.put(over_x(given_down))
    grad_mixed = collect(places, grad_attn, output_w).reshape(heads, HD, rows)
    grad_attn = jnp.concatenate(grad_attn, axis=0)

    if paired:
        (grad_mixed,) = after([grad_mixed], line.piece[0], scattered["gate"])
    dq, dkv = attend_back(count, tiles, q, kv, *masks, mixed, lse, grad_mixed)
    per = rows // TILE
    dkv_own = dkv[:per]
    moved = [dkv[d * per : (d + 1) * per].astype(low) for d in range(1, nz)]
    received = [shift(m, "ctx", nz, nz - 1 - d) for d, m in enumerate(moved)]
    if paired:
        (places,) = after([places], *moved)
        given_upper = weigh(places, normed_two, 1, half, dupper, 4, small)
        (places,) = after([places], given_upper)
        came_gate = over_x(given_gate)
        line.put(came_gate)
        gather("down")
        received = after(received, given_upper, line.piece[1], scattered["upper"], sums["down"])
        gather("gate", scattered["upper"])
        came_upper = over_x(given_upper)
        line.put(came_upper)
        attn_there, one_there, mixed_there = after(
            [theirs(grad_attn), theirs(normed_one), mixed_low], came_upper
        )
        attn_there, one_there = both_cores(attn_there), both_cores(one_there)
        mixed_there = over_x(mixed_there)
    else:
        line.put(spread(dot(mixed_low, grad_attn, 1, 0).astype(low), 1))
    for m in received:
        dkv_own = dkv_own + m.astype(high)
    dkv_own = jnp.transpose(dkv_own, (1, 0, 2)).reshape(2 * HD, rows)
    dq = turn(dq * 0.125, cosine, -sine).reshape(query_width, rows)
    dk = turn(dkv_own[None, :HD], cosine, -sine)[0]
    dqkv = jnp.concatenate([dq, dk, dkv_own[HD:]], axis=0).astype(low)
    first = project(places, [dqkv], [qkv_w], 0, 1)
    (places,) = after([places], first)
    keep, give = cut(first[None], 1)
    first_own, sent = scatter_rows(keep, give)
    if paired:
        (first_own,) = after([first_own], line.piece[2], sums["gate"])
        gather("upper", *sent)
        (places,) = after([places], *sent)
    else:
        qkv_grad = spread(dot(normed_one, dqkv, 0, 1).astype(low), 0)
    scale_own = scale_one[:block]
    inputs_own = inputs[:block]
    gain_one_sum = jnp.sum(first_own * inputs_own * scale_own, axis=0)
    input_own = grad_one + norm_back(inputs_own, scale_own, gain_one, first_own)
    input_low = input_own.astype(low)
    if paired:
        attn_there, mixed_there, one_there = after(
            [attn_there, mixed_there, one_there], input_low
        )
        output_grad = dot(mixed_low, mine(grad_attn), 1, 0) + dot(
            mixed_there, attn_there, 1, 0
        )
        line.put(output_grad.astype(low))
        (dqkv_there,) = after([over_x(dqkv)], input_low, line.piece[2])
        qkv_grad = (
            dot(mine(normed_one), dqkv, 0, 1) + dot(one_there, dqkv_there, 0, 1)
        ).astype(low)
    if not paired:
        gather("down")
        gather("gate")
        gather("upper")
    late = [sums["upper"]] if paired else []
    input_grad = place(order, gather_own(input_low, *late), high)
    ffn_own, _ = scatter_rows(ffn(0), ffn(1))
    activations = place(order, gather_own((one_own + ffn_own).astype(low)), low)

    gain_sums = sum_all(jnp.stack([gain_one_sum, gain_two_sum]), "tp", nt)
    if paired:
        gain_sums = mine(gain_sums) + over_x(theirs(gain_sums))
    else:
        gain_sums = lax.psum_scatter(gain_sums, "fsdp", scatter_dimension=1, tiled=True)
    upper_half, lower_half = jnp.split(qkv_grad, 2)
    line.put(upper_half)
    long = lower_half.shape[1]
    extra = -(-gain_sums.size // (16 * long)) * 16
    gain_sums = jnp.pad(gain_sums.reshape(-1), (0, extra * long - gain_sums.size))
    gain_sums = gain_sums.reshape(extra, long).astype(low)
    line.put(jnp.concatenate([lower_half, gain_sums], axis=0))
    assert nz == 4
    inner = ((here_z == 1) | (here_z == 2)).astype(jnp.int32)
    if paired:
        where = jnp.stack([inner, here_x * small, (1 - here_x) * big]).astype(jnp.int32)
    else:
        where = jnp.stack([inner, 0, 0]).astype(jnp.int32)
    def whole(i):
        return jnp.where(inner != 0, line.total[i], line.done[i])

    down_grad, gate_grad, upper_grad = (
        finish(where, axis, sums[name], *([line.total[i], line.done[i]] if paired else []))
        for i, (name, axis) in enumerate((("down", 0), ("gate", 1), ("upper", 1)))
    )
    output_grad = whole(-3).astype(high)
    qkv_grad = jnp.concatenate([whole(-2), whole(-1)[:-extra]], axis=0).astype(high)
    gain_sums = whole(-1)[-extra:].astype(high).reshape(-1)[: 2 * half].reshape(2, half)
    return (
        activations,
        input_grad,
        gain_sums[0],
        qkv_grad[:, :query_width],
        qkv_grad[:, query_width:],
        output_grad,
        gain_sums[1],
        gate_grad,
        upper_grad,
        down_grad,
    )


def solution(mesh):
    placed = (
        P(("fsdp", "ctx"), None),
        P("fsdp"),
        P("fsdp", "tp"),
        P("fsdp", "tp"),
        P("tp", "fsdp"),
        P("fsdp"),
        P("fsdp", "tp"),
        P("fsdp", "tp"),
        P("tp", "fsdp"),
        P("fsdp"),
        P("fsdp"),
        P(("fsdp", "ctx"), None),
    )
    sizes = (mesh.shape["fsdp"], mesh.shape["ctx"], mesh.shape["tp"])
    return jax.shard_map(
        functools.partial(per_device, sizes),
        mesh=mesh,
        in_specs=placed,
        out_specs=(
            P(("fsdp", "ctx"), None),
            P(("fsdp", "ctx"), None),
            P("fsdp"),
            P("fsdp", "tp"),
            P("fsdp", "tp"),
            P("tp", "fsdp"),
            P("fsdp"),
            P("fsdp", "tp"),
            P("fsdp", "tp"),
            P("tp", "fsdp"),
        ),
        check_vma=False,
    )
```

```python
import functools
import math

import jax
import jax.numpy as jnp
from jax import lax
from jax.experimental import pallas as pl
from jax.experimental.pallas import tpu as pltpu
from jax.sharding import PartitionSpec as P

HD = 64
TILE = 128
CODE = 4096
NEGATIVE = -1e30
epsilon = 1e-05
MIB = 2**20
SMALL = pl.CostEstimate(flops=1000000, bytes_accessed=100000, transcendentals=0)


def cost(microseconds):
    return pl.CostEstimate(
        flops=1000000, bytes_accessed=int(microseconds * SCALE * 3.69e6), transcendentals=0
    )


SCALE = 0.5


def dot(left, right, over_left, over_right):
    return lax.dot_general(
        left,
        right,
        (((over_left,), (over_right,)), ((), ())),
        preferred_element_type=jnp.float32,
    )


ORDER = (0, 2, 1, 3)


def swap(value, axis, distance, size):
    pairs = [(i, i ^ distance) for i in range(size)]
    return lax.ppermute(value, axis, pairs)


def shift(value, axis, size, distance):
    pairs = [(i, (i + distance) % size) for i in range(size)]
    return lax.ppermute(value, axis, pairs)


def over_x(value):
    return swap(value, "fsdp", 1, 2)


def over_y(value):
    return swap(value, "tp", 2, 4)


def over_core(value):
    return swap(value, "tp", 1, 4)


def add(left, right):
    return left.astype(jnp.float32) + right.astype(jnp.float32)


def cut(value, axis=0):
    keep, give = jnp.split(value, 2, axis=axis)
    return keep, give.astype(jnp.bfloat16)


def scatter_rows(keep, give, between=None):
    part = add(keep, over_core(give)).astype(jnp.bfloat16)
    if part.shape[0] == 1:
        keep, give = cut(part[0])
        return add(keep, over_y(give)), [give]
    left, right = jnp.split(part, 2, axis=2)
    keep_left, give_left = cut(left)
    keep_right, give_right = cut(right, 1)
    from_x, from_y = over_x(give_left), over_y(give_right)
    if between:
        from_x, from_y = after([from_x, from_y], *between([give_left, give_right]))
    left = add(keep_left, from_x)[0]
    right = add(keep_right, from_y)
    keep_left, give_left = cut(left)
    keep_right, give_right = cut(right)
    left = add(keep_left, over_y(give_left))
    right = add(keep_right, over_x(give_right))[0]
    return jnp.concatenate([left, right], axis=1), [give_left, give_right]


def both_cores(rows):
    first = over_x(rows[: rows.shape[0] // 2])
    return jnp.concatenate([first, over_core(first)], axis=0)


def gather_own(rows, *tokens):
    first = jnp.concatenate([rows, over_y(rows)], axis=0)
    if tokens:
        (first,) = after([first], *tokens)
    return first, over_core(first)


def gather_pair(rows, early=(), late=()):
    left, right = jnp.split(rows, 2, axis=1)
    left = jnp.stack([left, over_x(left)])
    right = jnp.concatenate([right, over_y(right)], axis=0)
    if early:
        left, right = after([left, right], *early)
    left = jnp.concatenate([left, over_y(left)], axis=1)
    right = jnp.stack([right, over_x(right)])
    first = jnp.concatenate([left, right], axis=2)
    if late:
        (first,) = after([first], *late)
    return first, over_core(first)


def sum_all(value, axis, size):
    distance = 1
    while distance < size:
        value = value + swap(value, axis, distance, size)
        distance *= 2
    return value


class Line:
    def __init__(self):
        self.piece, self.came, self.total, self.done = [], [], [], []

    def start(self, piece):
        k = len(self.piece)
        before = ((self.came, k - 1), (self.total, k - 2), (self.done, k - 3))
        earlier = [v[i] for v, i in before if i >= 0]
        if earlier:
            (piece,) = after([piece], *earlier)
        self.piece.append(piece)

    def land(self, *hold):
        piece = self.piece[len(self.came)]
        came = lax.ppermute(piece, "ctx", [(0, 1), (3, 2)])
        if hold:
            (came,) = after([came], *hold)
        self.came.append(came)
        inward = piece + came
        self.total.append(inward + lax.ppermute(inward, "ctx", [(1, 2), (2, 1)]))
        self.done.append(lax.ppermute(self.total[-1], "ctx", [(1, 0), (2, 3)]))

    def put(self, piece):
        self.start(piece)
        self.land()


def attend_kernel(
    heads, count, tiles, q, kv, q_code, q_base, k_code, mixed, lse, top, total, acc
):
    step = pl.program_id(0)
    top[...] = jnp.full_like(top, NEGATIVE)
    total[...] = jnp.zeros_like(total)
    acc[...] = jnp.zeros_like(acc)
    code, base = q_code[...], q_base[...]

    def body(j, carry):
        tile = tiles[step, j]
        keys = kv[tile, :HD]
        values = kv[tile, HD:]
        key_code = k_code[tile]
        allowed = (key_code <= code) & (key_code >= base)
        for h in range(heads):
            scores = jnp.where(allowed, dot(keys, q[h], 0, 0), NEGATIVE)
            before = top[h : h + 1]
            highest = jnp.maximum(before, jnp.max(scores, axis=0, keepdims=True))
            probs = jnp.exp(scores - highest)
            fade = jnp.exp(before - highest)
            top[h : h + 1] = highest
            total[h : h + 1] = total[h : h + 1] * fade + jnp.sum(probs, axis=0, keepdims=True)
            acc[h] = acc[h] * fade + dot(values, probs.astype(jnp.bfloat16), 1, 0)
        return carry

    lax.fori_loop(0, count[step], body, 0)
    sums = total[...]
    lse[...] = top[...] + jnp.log(sums)
    inverse = 1.0 / sums
    for h in range(heads):
        mixed[h] = acc[h] * inverse[h : h + 1]


def attend(count, tiles, q, kv, q_code, q_base, k_code):
    heads, _, rows = q.shape
    stack = pl.BlockSpec(kv.shape, lambda i, *_: (0, 0, 0))
    codes = pl.BlockSpec(k_code.shape, lambda i, *_: (0, 0, 0))
    line = pl.BlockSpec((1, TILE), lambda i, *_: (0, i))
    block = pl.BlockSpec((heads, HD, TILE), lambda i, *_: (0, 0, i))
    return pl.pallas_call(
        functools.partial(attend_kernel, heads),
        grid_spec=pltpu.PrefetchScalarGridSpec(
            num_scalar_prefetch=2,
            grid=(rows // TILE,),
            in_specs=[block, stack, line, line, codes],
            out_specs=[block, pl.BlockSpec((heads, TILE), lambda i, *_: (0, i))],
            scratch_shapes=[
                pltpu.VMEM((heads, TILE), jnp.float32),
                pltpu.VMEM((heads, TILE), jnp.float32),
                pltpu.VMEM((heads, HD, TILE), jnp.float32),
            ],
        ),
        out_shape=[
            jax.ShapeDtypeStruct((heads, HD, rows), jnp.float32),
            jax.ShapeDtypeStruct((heads, rows), jnp.float32),
        ],
        compiler_params=pltpu.CompilerParams(vmem_limit_bytes=60 * MIB),
        cost_estimate=SMALL,
    )(count, tiles, q, kv, q_code, q_base, k_code)


def attend_back_kernel(
    heads, count, tiles, q, kv, q_code, q_base, k_code, mixed, lse, upstream, dq, dkv, centre
):
    step = pl.program_id(0)

    @pl.when(step == 0)
    def _():
        dkv[...] = jnp.zeros_like(dkv)

    dq[...] = jnp.zeros_like(dq)
    code, base = q_code[...], q_base[...]
    for h in range(heads):
        centre[h : h + 1] = jnp.sum(
            mixed[h] * upstream[h].astype(jnp.float32), axis=0, keepdims=True
        )

    def body(j, carry):
        tile = tiles[step, j]
        keys = kv[tile, :HD]
        values = kv[tile, HD:]
        key_code = k_code[tile]
        allowed = (key_code <= code) & (key_code >= base)
        key_term = dkv[tile, :HD]
        value_term = dkv[tile, HD:]
        for h in range(heads):
            scores = dot(keys, q[h], 0, 0) - lse[h : h + 1]
            probs = jnp.exp(jnp.where(allowed, scores, NEGATIVE))
            grad_probs = dot(values, upstream[h], 0, 0)
            grad_scores = (probs * (grad_probs - centre[h : h + 1])).astype(jnp.bfloat16)
            value_term = value_term + dot(upstream[h], probs.astype(jnp.bfloat16), 1, 1)
            key_term = key_term + dot(q[h], grad_scores, 1, 1)
            dq[h] += dot(keys, grad_scores, 1, 0)
        dkv[tile, :HD] = key_term
        dkv[tile, HD:] = value_term
        return carry

    lax.fori_loop(0, count[step], body, 0)


def attend_back(count, tiles, q, kv, q_code, q_base, k_code, mixed, lse, upstream):
    heads, _, rows = q.shape
    stack = pl.BlockSpec(kv.shape, lambda i, *_: (0, 0, 0))
    codes = pl.BlockSpec(k_code.shape, lambda i, *_: (0, 0, 0))
    line = pl.BlockSpec((1, TILE), lambda i, *_: (0, i))
    block = pl.BlockSpec((heads, HD, TILE), lambda i, *_: (0, 0, i))
    return pl.pallas_call(
        functools.partial(attend_back_kernel, heads),
        grid_spec=pltpu.PrefetchScalarGridSpec(
            num_scalar_prefetch=2,
            grid=(rows // TILE,),
            in_specs=[
                block,
                stack,
                line,
                line,
                codes,
                block,
                pl.BlockSpec((heads, TILE), lambda i, *_: (0, i)),
                block,
            ],
            out_specs=[block, stack],
            scratch_shapes=[pltpu.VMEM((heads, TILE), jnp.float32)],
        ),
        out_shape=[
            jax.ShapeDtypeStruct((heads, HD, rows), jnp.float32),
            jax.ShapeDtypeStruct(kv.shape, jnp.float32),
        ],
        compiler_params=pltpu.CompilerParams(vmem_limit_bytes=60 * MIB),
        cost_estimate=cost(24),
    )(count, tiles, q, kv, q_code, q_base, k_code, mixed, lse, upstream)


def plan_tiles(q_code, q_base, k_code):
    rows, keys = q_code.shape[0], k_code.shape[0]
    allowed = (k_code[None, :] <= q_code[:, None]) & (k_code[None, :] >= q_base[:, None])
    used = jnp.any(allowed.reshape(rows // TILE, TILE, keys // TILE, TILE), axis=(1, 3))
    place = jnp.cumsum(used.astype(jnp.int32), axis=1) - 1
    ladder = jnp.arange(keys // TILE)
    hit = used[:, :, None] & (place[:, :, None] == ladder[None, None, :])
    tiles = jnp.sum(jnp.where(hit, ladder[None, :, None], 0), axis=1).astype(jnp.int32)
    return jnp.sum(used.astype(jnp.int32), axis=1), tiles


def nothing(*refs):
    pass


def after(values, *tokens):
    anywhere = pl.BlockSpec(memory_space=pl.ANY)
    return pl.pallas_call(
        nothing,
        in_specs=[anywhere] * (len(values) + len(tokens)),
        out_specs=[anywhere] * len(values),
        out_shape=[jax.ShapeDtypeStruct(v.shape, v.dtype) for v in values],
        input_output_aliases={i: i for i in range(len(values))},
    )(*values, *tokens)


def outer_kernel(parts, places, upstream, *refs):
    pieces, out = refs[:parts], refs[parts]
    total = 0.0
    for i in range(parts):
        columns = pl.ds(pl.multiple_of(places[i], TILE), pieces[i].shape[1])
        total = total + dot(upstream[:, columns], pieces[i][...], 1, 1)
    out[...] = total


def outer(places, upstream, down_w):
    count, width = upstream.shape
    units = down_w[0].shape[0]
    block = 256
    flat = [pl.BlockSpec((block, w.shape[1]), lambda i, *_: (i, 0)) for w in down_w]
    return pl.pallas_call(
        functools.partial(outer_kernel, len(down_w)),
        grid_spec=pltpu.PrefetchScalarGridSpec(
            num_scalar_prefetch=1,
            grid=(pl.cdiv(units, block),),
            in_specs=[pl.BlockSpec((count, width), lambda i, *_: (0, 0)), *flat],
            out_specs=pl.BlockSpec((count, block), lambda i, *_: (0, i)),
        ),
        out_shape=jax.ShapeDtypeStruct((count, units), jnp.float32),
        compiler_params=pltpu.CompilerParams(vmem_limit_bytes=60 * MIB),
        cost_estimate=SMALL,
    )(places, upstream, *down_w)


def middle_kernel(parts, places, rows, grads, *refs):
    pieces, (hidden, dgate, dupper) = refs[: 2 * parts], refs[2 * parts :]
    gate = upper = 0.0
    for i in range(parts):
        columns = pl.ds(pl.multiple_of(places[i], TILE), pieces[i].shape[0])
        left = rows[:, columns]
        gate = gate + dot(left, pieces[i][...], 1, 0)
        upper = upper + dot(left, pieces[parts + i][...], 1, 0)
    grad = grads[...]
    sigma = 1.0 / (1.0 + jnp.exp(-gate))
    swish = gate * sigma
    hidden[...] = (swish * upper).astype(jnp.bfloat16)
    dgate[...] = (grad * upper * sigma * (1.0 + gate * (1.0 - sigma))).astype(jnp.bfloat16)
    dupper[...] = (grad * swish).astype(jnp.bfloat16)


def middle(places, rows, grads, gate_w, upper_w):
    parts = len(gate_w)
    count, width = rows.shape
    units = gate_w[0].shape[1]
    block = 256
    out = pl.BlockSpec((count, block), lambda i, *_: (0, i))
    tall = [pl.BlockSpec((w.shape[0], block), lambda i, *_: (0, i)) for w in gate_w]
    return pl.pallas_call(
        functools.partial(middle_kernel, parts),
        grid_spec=pltpu.PrefetchScalarGridSpec(
            num_scalar_prefetch=1,
            grid=(pl.cdiv(units, block),),
            in_specs=[pl.BlockSpec((count, width), lambda i, *_: (0, 0)), out, *tall, *tall],
            out_specs=[out, out, out],
        ),
        out_shape=[jax.ShapeDtypeStruct((count, units), jnp.bfloat16)] * 3,
        compiler_params=pltpu.CompilerParams(vmem_limit_bytes=60 * MIB),
        cost_estimate=cost(9),
    )(places, rows, grads, *gate_w, *upper_w)


def project_kernel(parts, factors, steps, over_left, over_right, skip, places, *refs):
    lefts, pieces, out = refs[:factors], refs[factors:-1], refs[-1]
    step = pl.program_id(0)

    def one(i, start):
        total = 0.0
        for f in range(factors):
            left, right = lefts[f], pieces[f * parts + i]
            left = left[:, start:] if over_left else left[start:]
            right = right[:, start:] if over_right else right[start:]
            total = total + dot(left, right, over_left, over_right)
        out[...] = total.astype(out.dtype)

    for i in range(parts):
        here = (step >= i * steps) & (step < (i + 1) * steps)
        if skip:
            pl.when(here & (places[parts] == 0))(functools.partial(one, i, 0))
            pl.when(here & (places[parts] != 0))(functools.partial(one, i, skip))
        else:
            pl.when(here)(functools.partial(one, i, 0))


def project(places, lefts, weights, over_left, over_right, skip=0):
    parts, factors = len(weights[0]), len(lefts)
    axis = 1 - over_right
    size = weights[0][0].shape[axis]
    block = min(512, size)
    steps = size // block
    depth = weights[0][0].shape[over_right]
    count = lefts[0].shape[1 - over_left]

    def spec(i):
        at = lambda s: jnp.clip(s - i * steps, 0, steps - 1)
        if axis == 0:
            return pl.BlockSpec((block, depth), lambda s, *_: (at(s), 0))
        return pl.BlockSpec((depth, block), lambda s, *_: (0, at(s)))

    return pl.pallas_call(
        functools.partial(
            project_kernel, parts, factors, steps, over_left, over_right, skip
        ),
        grid_spec=pltpu.PrefetchScalarGridSpec(
            num_scalar_prefetch=1,
            grid=(parts * steps,),
            in_specs=[pl.BlockSpec(v.shape, lambda s, *_: (0, 0)) for v in lefts]
            + [spec(i) for _ in range(factors) for i in range(parts)],
            out_specs=pl.BlockSpec(
                (count, block), lambda s, p: (0, p[s // steps] // block + s % steps)
            ),
        ),
        out_shape=jax.ShapeDtypeStruct((count, parts * size), jnp.bfloat16),
        compiler_params=pltpu.CompilerParams(vmem_limit_bytes=60 * MIB),
        cost_estimate=cost(3 * len(lefts)),
    )(places, *lefts, *[w for weight in weights for w in weight])


def collect_kernel(parts, sets, places, *refs):
    rows, pieces, out = refs[:sets], refs[sets:-1], refs[-1]
    at = 0
    for block in rows:
        total = 0.0
        for i in range(parts):
            columns = pl.ds(pl.multiple_of(places[i], TILE), pieces[i].shape[1])
            total = total + dot(pieces[i][...], block[:, columns], 1, 1)
        out[:, at : at + block.shape[0]] = total.astype(out.dtype)
        at += block.shape[0]


def collect(places, rows, pieces):
    parts, count = len(pieces), sum(v.shape[0] for v in rows)
    units = pieces[0].shape[0]
    block = 256
    specs = [pl.BlockSpec((block, w.shape[1]), lambda i, *_: (i, 0)) for w in pieces]
    return pl.pallas_call(
        functools.partial(collect_kernel, parts, len(rows)),
        grid_spec=pltpu.PrefetchScalarGridSpec(
            num_scalar_prefetch=1,
            grid=(units // block,),
            in_specs=[pl.BlockSpec(v.shape, lambda i, *_: (0, 0)) for v in rows] + specs,
            out_specs=pl.BlockSpec((block, count), lambda i, *_: (i, 0)),
        ),
        out_shape=jax.ShapeDtypeStruct((units, count), jnp.bfloat16),
        compiler_params=pltpu.CompilerParams(vmem_limit_bytes=60 * MIB),
        cost_estimate=cost(5),
    )(places, *rows, *pieces)


def weigh_kernel(parts, at_left, at_right, wide, places, *refs):
    lefts, rights, out = refs[:parts], refs[parts:-1], refs[-1]
    columns = pl.ds(pl.multiple_of(places[at_right], TILE), wide)
    total = 0.0
    for left, right in zip(lefts, rights):
        total = total + dot(left[...], right[:, columns], 0, 0)
    out[...] = total.astype(out.dtype)


def weigh(places, lefts, at_left, tall, rights, at_right, wide):
    parts = len(lefts)
    count = lefts[0].shape[0]
    block = TILE if tall % 256 or lefts[0].shape[1] % 256 else 256
    return pl.pallas_call(
        functools.partial(weigh_kernel, parts, at_left, at_right, wide),
        grid_spec=pltpu.PrefetchScalarGridSpec(
            num_scalar_prefetch=1,
            grid=(tall // block,),
            in_specs=[
                pl.BlockSpec((count, block), lambda i, p: (0, p[at_left] // block + i))
                for _ in lefts
            ]
            + [pl.BlockSpec(v.shape, lambda i, p: (0, 0)) for v in rights],
            out_specs=pl.BlockSpec((block, wide), lambda i, p: (i, 0)),
        ),
        out_shape=jax.ShapeDtypeStruct((tall, wide), jnp.bfloat16),
        compiler_params=pltpu.CompilerParams(vmem_limit_bytes=60 * MIB),
        cost_estimate=cost(6),
    )(places, *lefts, *rights)


def plus_kernel(left, right, out):
    out[...] = (left[...].astype(jnp.float32) + right[...].astype(jnp.float32)).astype(out.dtype)


def plus(left, right):
    rows, width = left.shape
    block = rows // 4 if rows % 64 == 0 else rows
    spec = pl.BlockSpec((block, width), lambda i: (i, 0))
    return pl.pallas_call(
        plus_kernel,
        grid=(rows // block,),
        in_specs=[spec, spec],
        out_specs=spec,
        out_shape=jax.ShapeDtypeStruct(left.shape, left.dtype),
        compiler_params=pltpu.CompilerParams(vmem_limit_bytes=60 * MIB),
        cost_estimate=SMALL,
    )(left, right)


def entry_kernel(parts, query_steps, places, rows, cosine, sine, *refs):
    pieces, (q, kv) = refs[:parts], refs[parts:]
    step = pl.program_id(0)
    total = 0.0
    for i in range(parts):
        columns = pl.ds(pl.multiple_of(places[i], TILE), pieces[i].shape[0])
        total = total + dot(pieces[i][...], rows[:, columns], 0, 1)
    half = HD // 2

    def turned(start):
        former, latter = total[start : start + half], total[start + half : start + HD]
        return jnp.concatenate(
            [
                former * cosine[...] - latter * sine[...],
                latter * cosine[...] + former * sine[...],
            ],
            axis=0,
        ).astype(jnp.bfloat16)

    @pl.when(step < query_steps)
    def _():
        for start in (0, HD):
            q[start : start + HD] = turned(start) * 0.125

    @pl.when(step == query_steps)
    def _():
        keys = turned(0)
        values = total[HD:].astype(jnp.bfloat16)
        for j in range(kv.shape[0]):
            columns = slice(j * TILE, (j + 1) * TILE)
            kv[j, :HD] = keys[:, columns]
            kv[j, HD:] = values[:, columns]


def entry(places, rows, cosine, sine, pieces):
    parts = len(pieces)
    count, width = rows.shape
    steps = pieces[0].shape[1] // TILE - 1
    table = pl.BlockSpec(cosine.shape, lambda i, *_: (0, 0))
    return pl.pallas_call(
        functools.partial(entry_kernel, parts, steps),
        grid_spec=pltpu.PrefetchScalarGridSpec(
            num_scalar_prefetch=1,
            grid=(steps + 1,),
            in_specs=[pl.BlockSpec((count, width), lambda i, *_: (0, 0)), table, table]
            + [pl.BlockSpec((w.shape[0], TILE), lambda i, *_: (0, i)) for w in pieces],
            out_specs=[
                pl.BlockSpec((TILE, count), lambda i, *_: (jnp.minimum(i, steps - 1), 0)),
                pl.BlockSpec((count // TILE, TILE, TILE), lambda i, *_: (0, 0, 0)),
            ],
        ),
        out_shape=[
            jax.ShapeDtypeStruct((steps * TILE, count), jnp.bfloat16),
            jax.ShapeDtypeStruct((count // TILE, TILE, TILE), jnp.bfloat16),
        ],
        compiler_params=pltpu.CompilerParams(vmem_limit_bytes=60 * MIB),
        cost_estimate=SMALL,
    )(places, rows, cosine, sine, *pieces)


def place_kernel(order, first, second, out):
    step = pl.program_id(0)

    @pl.when(step < 2)
    def _():
        out[...] = first[...].astype(out.dtype)

    @pl.when(step >= 2)
    def _():
        out[...] = second[...].astype(out.dtype)


def place(order, halves, dtype):
    size, width = halves[0].shape[0] // 2, halves[0].shape[1]
    return pl.pallas_call(
        place_kernel,
        grid_spec=pltpu.PrefetchScalarGridSpec(
            num_scalar_prefetch=1,
            grid=(4,),
            in_specs=[
                pl.BlockSpec((size, width), lambda i, *_: (jnp.minimum(i, 1), 0)),
                pl.BlockSpec((size, width), lambda i, *_: (jnp.maximum(i - 2, 0), 0)),
            ],
            out_specs=pl.BlockSpec((size, width), lambda i, o: (o[i], 0)),
        ),
        out_shape=jax.ShapeDtypeStruct((4 * size, width), dtype),
        compiler_params=pltpu.CompilerParams(vmem_limit_bytes=60 * MIB),
        cost_estimate=cost(5),
    )(order, *halves)


def finish_kernel(axis, where, kept, *refs):
    out = refs[-1]
    if len(refs) == 1:
        out[...] = kept[...].astype(jnp.float32)
        return
    came = jnp.where(where[0] != 0, refs[0][...], refs[1][...])
    for i, piece in enumerate((kept[...], came)):
        at = pl.ds(pl.multiple_of(where[1 + i], TILE), piece.shape[axis])
        if axis == 0:
            out[at] = piece.astype(jnp.float32)
        else:
            out[:, at] = piece.astype(jnp.float32)


def finish(where, axis, kept, *came):
    shape = list(kept.shape)
    shape[axis] += came[0].shape[axis] if came else 0
    block = 256 if shape[1 - axis] % 256 == 0 else shape[1 - axis]

    def spec(size):
        if axis == 0:
            return pl.BlockSpec((size, block), lambda s, *_: (0, s))
        return pl.BlockSpec((block, size), lambda s, *_: (s, 0))

    return pl.pallas_call(
        functools.partial(finish_kernel, axis),
        grid_spec=pltpu.PrefetchScalarGridSpec(
            num_scalar_prefetch=1,
            grid=(shape[1 - axis] // block,),
            in_specs=[spec(p.shape[axis]) for p in (kept, *came)],
            out_specs=spec(shape[axis]),
        ),
        out_shape=jax.ShapeDtypeStruct(shape, jnp.float32),
        compiler_params=pltpu.CompilerParams(vmem_limit_bytes=60 * MIB),
        cost_estimate=cost(6),
    )(where, kept, *came)


def rms_scale(values):
    return lax.rsqrt(jnp.mean(values * values, axis=-1, keepdims=True) + epsilon)


def norm_back(values, scale, gain, upstream):
    weighted = upstream * gain
    return scale * weighted - values * scale**3 * jnp.mean(
        values * weighted, axis=-1, keepdims=True
    )


def turn(values, cosine, sine):
    half = HD // 2
    former, latter = values[:, :half], values[:, half:]
    return jnp.concatenate(
        [former * cosine - latter * sine, latter * cosine + former * sine], axis=1
    )


def per_device(
    sizes,
    tokens,
    first_gain,
    query_weight,
    keyval_weight,
    output_weight,
    second_gain,
    gate_weight,
    up_weight,
    down_weight,
    segment_ids,
    positions,
    cotangent,
):
    nx, nz, nt = sizes
    low, high = jnp.bfloat16, jnp.float32
    rows, width = tokens.shape
    block = rows // nt
    half = width // nx
    here_x, here_z, here_t = (lax.axis_index(a) for a in ("fsdp", "ctx", "tp"))
    paired = nx == 2
    assert nt == 4 and block % TILE == 0 and keyval_weight.shape[1] == 2 * HD
    order = jnp.stack([here_t ^ k for k in ORDER]).astype(jnp.int32)

    def arranged(whole, axis=0):
        return jnp.concatenate(
            [
                lax.dynamic_slice_in_dim(whole, (here_t ^ k) * block, block, axis)
                for k in ORDER
            ],
            axis=axis,
        )

    def part(whole, start, size, axis):
        return lax.dynamic_slice_in_dim(whole, start, size, axis)

    def mine(whole):
        return part(whole, here_x * half, half, 1)

    def theirs(whole):
        return part(whole, (1 - here_x) * half, half, 1)

    units = gate_weight.shape[1]
    query_width = query_weight.shape[1]
    heads = query_width // HD
    qkv_shard = jnp.concatenate([query_weight, keyval_weight], axis=1)
    gain_shards = jnp.stack([first_gain, second_gain])
    if paired:
        big = (units // TILE + 1) // 2 * TILE
        small = units - big
        spare = big - small
        places = jnp.stack(
            [here_x * half, (1 - here_x) * half, here_x, 0 * here_x, here_x * spare]
        ).astype(jnp.int32)
        at, at_theirs = here_x * small, (1 - here_x) * small
        gains_there = over_x(gain_shards)
        gains = jnp.where(
            here_x == 0,
            jnp.concatenate([gain_shards, gains_there], axis=1),
            jnp.concatenate([gains_there, gain_shards], axis=1),
        )
        qkv_w = (qkv_shard, over_x(qkv_shard))
        output_w = (output_weight, over_x(after([output_weight], gains_there)[0]))
        fourth = half // nz

        def around(received):
            return lax.all_gather(received, "ctx", axis=0, tiled=True)

        def columns(weight):
            start = (here_z * fourth, at_theirs)
            piece = lax.dynamic_slice(weight, start, (fourth, big))
            return over_x(after([piece], gains_there)[0])

        gate_fourth, upper_fourth = columns(gate_weight), columns(up_weight)
        gate_own, upper_own = part(gate_weight, at, big, 1), part(up_weight, at, big, 1)
        down_w = (part(down_weight, at, big, 0), over_x(part(down_weight, at_theirs, big, 0)))
    else:
        spare = 0
        places = jnp.zeros((2,), jnp.int32)
        whole = lambda shard, dim: lax.all_gather(shard, "fsdp", axis=dim, tiled=True)
        gains = whole(gain_shards, 1)
        qkv_w, output_w = (whole(qkv_shard, 0),), (whole(output_weight, 1),)
        gate_w, upper_w = (whole(gate_weight, 0),), (whole(up_weight, 0),)
        down_w = (whole(down_weight, 1),)
    gains = gains.astype(high)
    gain_one, gain_two = gains[0], gains[1]

    codes = arranged((segment_ids * CODE + positions).reshape(nz, rows), 1)
    bases = arranged((segment_ids * CODE).reshape(nz, rows), 1)
    q_code = lax.dynamic_index_in_dim(codes, here_z, 0, False)
    q_base = lax.dynamic_index_in_dim(bases, here_z, 0, False)
    k_code = jnp.concatenate(
        [
            lax.dynamic_index_in_dim(codes, (here_z + nz - d) % nz, 0, False)
            for d in range(nz)
        ]
    )
    count, tiles = plan_tiles(q_code, q_base, k_code)
    k_wide = jnp.broadcast_to(k_code.reshape(-1, TILE, 1), (nz * rows // TILE, TILE, TILE))
    masks = (q_code[None], q_base[None], k_wide)
    spots = (q_code - q_base).astype(high)
    freqs = jnp.exp(jnp.arange(HD // 2).astype(high) * (-2.0 * math.log(10000.0) / HD))
    angles = freqs[:, None] * spots[None, :]
    cosine, sine = jnp.cos(angles), jnp.sin(angles)

    tokens = arranged(tokens)
    cotangent = arranged(cotangent)
    inputs = tokens.astype(high)
    scale_one = rms_scale(inputs)
    normed_one = (inputs * scale_one * gain_one).astype(low)
    q, kv = entry(places, normed_one, cosine, sine, qkv_w)
    q = q.reshape(heads, HD, rows)
    kv = jnp.concatenate([kv] + [shift(kv, "ctx", nz, d) for d in range(1, nz)], axis=0)
    mixed, lse = attend(count, tiles, q, kv, *masks)
    if paired:
        gate_fourth, upper_fourth = after([gate_fourth, upper_fourth], lse)
        gate_w = (gate_own, around(gate_fourth))
        upper_w = (upper_own, around(upper_fourth))

    mixed_low = mixed.reshape(query_width, rows).astype(low)
    attn = project(places, [mixed_low], [output_w], 0, 0)
    keep, give = cut(attn[None], 1)
    attn_own, _ = scatter_rows(keep, give)
    one_own = inputs[:block] + attn_own
    scale_two = rms_scale(one_own)
    normed_own = (one_own * scale_two * gain_two).astype(low)

    if paired:
        there = over_x(cotangent[:block])
        there = jnp.concatenate([there, over_y(there)], axis=0)
        upstream = [
            jnp.concatenate([c, t], axis=0)
            for c, t in zip(jnp.split(cotangent, 2), (there, over_core(there)))
        ]
        (normed_own,) = after([normed_own], *upstream, down_w[1], gate_w[1])
        grads = [outer(places, u, down_w) for u in upstream]
        normed_two = gather_pair(normed_own, [grads[0]], [grads[1], upper_w[1]])
    else:
        normed_two = gather_own(normed_own)
        upstream = jnp.split(cotangent, 2)
        grads = [outer(places, u, down_w) for u in upstream]
    normed_two = [v.reshape(-1, width) for v in normed_two]
    sets = 2 if paired else 1

    def spread(value, dim):
        return lax.psum_scatter(value, "fsdp", scatter_dimension=dim, tiled=True)

    def forward(i):
        return middle(places, normed_two[i], grads[i], gate_w, upper_w)

    def back(i):
        made = project(places, [dgate[i], dupper[i]], [gate_w, upper_w], 1, 1, spare)
        return made.reshape(sets, -1, width)

    def ffn(i):
        return project(places, [hidden[i]], [down_w], 1, 0, spare).reshape(sets, -1, width)

    line = Line()
    scattered, sums = {}, {}

    def scatter(name, piece):
        scattered[name] = lax.psum_scatter(piece, "ctx", scatter_dimension=0, tiled=True)

    def gather(name, *tokens):
        piece = scattered[name]
        if tokens:
            (piece,) = after([piece], *tokens)
        sums[name] = lax.all_gather(piece, "ctx", axis=0, tiled=True)

    hidden, dgate, dupper = [None, None], [None, None], [None, None]
    if paired:
        hidden[1], dgate[1], dupper[1] = forward(1)
        (places,) = after([places], hidden[1])
        grad_give = back(1)
        (places,) = after([places], grad_give)
        hidden[0], dgate[0], dupper[0] = forward(0)
        (places,) = after([places], hidden[0])
        kept_down = weigh(places, hidden, 3, big, upstream, 0, half)
        scatter("down", kept_down)
        (places,) = after([places], kept_down)
        grad_keep = back(0)
        kept = {}

        def between(sent):
            after_sent = after([places], grad_keep, *sent)[0]
            kept["gate"] = weigh(after_sent, normed_two, 0, half, dgate, 3, big)
            scatter("gate", kept["gate"])
            return [kept["gate"]]

        grad_own, sent = scatter_rows(grad_keep, grad_give, between)
        (places,) = after([places], kept["gate"], *sent)
        given_down = weigh(places, hidden, 4, small, upstream, 1, half)
        (places,) = after([places], given_down)
        (grad_own,) = after([grad_own], given_down)
    else:
        for i in range(2):
            hidden[i], dgate[i], dupper[i] = forward(i)
        weight_grad = lambda lefts, rights: sum(
            dot(left, right, 0, 0) for left, right in zip(lefts, rights)
        ).astype(low)
        scatter("down", spread(weight_grad(hidden, upstream), 1))
        scatter("gate", spread(weight_grad(normed_two, dgate), 0))
        scatter("upper", spread(weight_grad(normed_two, dupper), 0))
        grad_own, _ = scatter_rows(back(0), back(1))
    grad_one = cotangent[:block].astype(high) + norm_back(
        one_own, scale_two, gain_two, grad_own
    )
    grad_one_low = grad_one.astype(low)
    gain_two_sum = jnp.sum(grad_own * one_own * scale_two, axis=0)
    grad_attn = gather_own(grad_one_low)
    if paired:
        (places,) = after([places], grad_one_low)
        kept_upper = weigh(places, normed_two, 0, half, dupper, 3, big)
        scatter("upper", kept_upper)
        (places,) = after([places], kept_upper)
        given_gate = weigh(places, normed_two, 1, half, dgate, 4, small)
        (places,) = after([places], given_gate)
        line.put(over_x(given_down))
    grad_mixed = collect(places, grad_attn, output_w).reshape(heads, HD, rows)
    grad_attn = jnp.concatenate(grad_attn, axis=0)

    if paired:
        (grad_mixed,) = after([grad_mixed], line.piece[0], scattered["gate"])
    dq, dkv = attend_back(count, tiles, q, kv, *masks, mixed, lse, grad_mixed)
    per = rows // TILE
    dkv_own = dkv[:per]
    moved = [dkv[d * per : (d + 1) * per].astype(low) for d in range(1, nz)]
    received = [shift(m, "ctx", nz, nz - 1 - d) for d, m in enumerate(moved)]
    if paired:
        (places,) = after([places], *moved)
        given_upper = weigh(places, normed_two, 1, half, dupper, 4, small)
        (places,) = after([places], given_upper)
        came_gate = over_x(given_gate)
        line.start(came_gate)
        gather("down")
        received = after(received, given_upper, line.piece[1], scattered["upper"], sums["down"])
        gather("gate", scattered["upper"])
        came_upper = over_x(given_upper)
        attn_there, one_there, mixed_there = after(
            [theirs(grad_attn), theirs(normed_one), mixed_low], came_upper
        )
    else:
        line.put(spread(dot(mixed_low, grad_attn, 1, 0).astype(low), 1))
    for m in received:
        dkv_own = dkv_own + m.astype(high)
    dkv_own = jnp.transpose(dkv_own, (1, 0, 2)).reshape(2 * HD, rows)
    dq = turn(dq * 0.125, cosine, -sine).reshape(query_width, rows)
    dk = turn(dkv_own[None, :HD], cosine, -sine)[0]
    dqkv = jnp.concatenate([dq, dk, dkv_own[HD:]], axis=0).astype(low)
    first = project(places, [dqkv], [qkv_w], 0, 1)
    (places,) = after([places], first)
    keep, give = cut(first[None], 1)
    first_own, sent = scatter_rows(keep, give)
    if paired:
        line.land(first_own)
        line.put(came_upper)
        gather("upper", *sent)
        (places,) = after([places], *sent)
    else:
        qkv_grad = spread(dot(normed_one, dqkv, 0, 1).astype(low), 0)
    scale_own = scale_one[:block]
    inputs_own = inputs[:block]
    gain_one_sum = jnp.sum(first_own * inputs_own * scale_own, axis=0)
    input_own = grad_one + norm_back(inputs_own, scale_own, gain_one, first_own)
    input_low = input_own.astype(low)
    if paired:
        attn_there, mixed_there, one_there = after(
            [attn_there, mixed_there, one_there], input_low
        )
        attn_there, one_there = both_cores(attn_there), both_cores(one_there)
        mixed_there = over_x(mixed_there)
        output_grad = dot(mixed_low, mine(grad_attn), 1, 0) + dot(
            mixed_there, attn_there, 1, 0
        )
        line.put(output_grad.astype(low))
        (dqkv_there,) = after([over_x(dqkv)], input_low)
        qkv_grad = (
            dot(mine(normed_one), dqkv, 0, 1) + dot(one_there, dqkv_there, 0, 1)
        ).astype(low)
    if not paired:
        gather("down")
        gather("gate")
        gather("upper")
    late = [line.piece[2]] if paired else []
    (places,) = after([places], input_low)
    if paired:
        (places,) = after([places], sums["gate"])
    input_grad = place(order, gather_own(input_low, *late), high)
    ffn_give = ffn(1)
    if paired:
        (places,) = after([places], ffn_give, sums["upper"])
    ffn_own, _ = scatter_rows(ffn(0), ffn_give)
    activations = place(order, gather_own((one_own + ffn_own).astype(low)), low)

    gain_sums = sum_all(jnp.stack([gain_one_sum, gain_two_sum]), "tp", nt)
    if paired:
        gain_sums = mine(gain_sums) + over_x(theirs(gain_sums))
    else:
        gain_sums = lax.psum_scatter(gain_sums, "fsdp", scatter_dimension=1, tiled=True)
    upper_half, lower_half = jnp.split(qkv_grad, 2)
    line.put(upper_half)
    long = lower_half.shape[1]
    extra = -(-gain_sums.size // (16 * long)) * 16
    gain_sums = jnp.pad(gain_sums.reshape(-1), (0, extra * long - gain_sums.size))
    gain_sums = gain_sums.reshape(extra, long).astype(low)
    line.put(jnp.concatenate([lower_half, gain_sums], axis=0))
    assert nz == 4
    inner = ((here_z == 1) | (here_z == 2)).astype(jnp.int32)
    if paired:
        where = jnp.stack([inner, here_x * small, (1 - here_x) * big]).astype(jnp.int32)
    else:
        where = jnp.stack([inner, 0, 0]).astype(jnp.int32)
    def whole(i):
        return jnp.where(inner != 0, line.total[i], line.done[i])

    down_grad, gate_grad, upper_grad = (
        finish(where, axis, sums[name], *([line.total[i], line.done[i]] if paired else []))
        for i, (name, axis) in enumerate((("down", 0), ("gate", 1), ("upper", 1)))
    )
    output_grad = whole(-3).astype(high)
    halves = (whole(-2).astype(high), whole(-1)[:-extra].astype(high))
    query_grad = jnp.concatenate([v[:, :query_width] for v in halves], axis=0)
    keyval_grad = jnp.concatenate([v[:, query_width:] for v in halves], axis=0)
    gain_sums = whole(-1)[-extra:].astype(high).reshape(-1)[: 2 * half].reshape(2, half)
    return (
        activations,
        input_grad,
        gain_sums[0],
        query_grad,
        keyval_grad,
        output_grad,
        gain_sums[1],
        gate_grad,
        upper_grad,
        down_grad,
    )


def solution(mesh):
    placed = (
        P(("fsdp", "ctx"), None),
        P("fsdp"),
        P("fsdp", "tp"),
        P("fsdp", "tp"),
        P("tp", "fsdp"),
        P("fsdp"),
        P("fsdp", "tp"),
        P("fsdp", "tp"),
        P("tp", "fsdp"),
        P("fsdp"),
        P("fsdp"),
        P(("fsdp", "ctx"), None),
    )
    sizes = (mesh.shape["fsdp"], mesh.shape["ctx"], mesh.shape["tp"])
    return jax.shard_map(
        functools.partial(per_device, sizes),
        mesh=mesh,
        in_specs=placed,
        out_specs=(
            P(("fsdp", "ctx"), None),
            P(("fsdp", "ctx"), None),
            P("fsdp"),
            P("fsdp", "tp"),
            P("fsdp", "tp"),
            P("tp", "fsdp"),
            P("fsdp"),
            P("fsdp", "tp"),
            P("fsdp", "tp"),
            P("tp", "fsdp"),
        ),
        check_vma=False,
    )
```

```python
import functools
import math

import jax
import jax.numpy as jnp
from jax import lax
from jax.experimental import pallas as pl
from jax.experimental.pallas import tpu as pltpu
from jax.sharding import PartitionSpec as P

HD = 64
TILE = 128
CODE = 4096
NEGATIVE = -1e30
epsilon = 1e-05
MIB = 2**20
SMALL = pl.CostEstimate(flops=1000000, bytes_accessed=100000, transcendentals=0)


def cost(microseconds):
    return pl.CostEstimate(
        flops=1000000, bytes_accessed=int(microseconds * SCALE * 3.69e6), transcendentals=0
    )


SCALE = 0.5


def dot(left, right, over_left, over_right):
    return lax.dot_general(
        left,
        right,
        (((over_left,), (over_right,)), ((), ())),
        preferred_element_type=jnp.float32,
    )


ORDER = (0, 2, 1, 3)


def swap(value, axis, distance, size):
    pairs = [(i, i ^ distance) for i in range(size)]
    return lax.ppermute(value, axis, pairs)


def shift(value, axis, size, distance):
    pairs = [(i, (i + distance) % size) for i in range(size)]
    return lax.ppermute(value, axis, pairs)


def over_x(value):
    return swap(value, "fsdp", 1, 2)


def over_y(value):
    return swap(value, "tp", 2, 4)


def over_core(value):
    return swap(value, "tp", 1, 4)


def add(left, right):
    return left.astype(jnp.float32) + right.astype(jnp.float32)


def cut(value, axis=0):
    keep, give = jnp.split(value, 2, axis=axis)
    return keep, give.astype(jnp.bfloat16)


def scatter_rows(keep, give, between=None):
    part = add(keep, over_core(give)).astype(jnp.bfloat16)
    if part.shape[0] == 1:
        keep, give = cut(part[0])
        return add(keep, over_y(give)), [give]
    left, right = jnp.split(part, 2, axis=2)
    keep_left, give_left = cut(left)
    keep_right, give_right = cut(right, 1)
    from_x, from_y = over_x(give_left), over_y(give_right)
    if between:
        from_x, from_y = after([from_x, from_y], *between([give_left, give_right]))
    left = add(keep_left, from_x)[0]
    right = add(keep_right, from_y)
    keep_left, give_left = cut(left)
    keep_right, give_right = cut(right)
    left = add(keep_left, over_y(give_left))
    right = add(keep_right, over_x(give_right))[0]
    return jnp.concatenate([left, right], axis=1), [give_left, give_right]


def both_cores(rows):
    first = over_x(rows[: rows.shape[0] // 2])
    return jnp.concatenate([first, over_core(first)], axis=0)


def gather_own(rows, *tokens):
    first = jnp.concatenate([rows, over_y(rows)], axis=0)
    if tokens:
        (first,) = after([first], *tokens)
    return first, over_core(first)


def gather_pair(rows, early=(), late=()):
    left, right = jnp.split(rows, 2, axis=1)
    left = jnp.stack([left, over_x(left)])
    right = jnp.concatenate([right, over_y(right)], axis=0)
    if early:
        left, right = after([left, right], *early)
    left = jnp.concatenate([left, over_y(left)], axis=1)
    right = jnp.stack([right, over_x(right)])
    first = jnp.concatenate([left, right], axis=2)
    if late:
        (first,) = after([first], *late)
    return first, over_core(first)


def sum_all(value, axis, size):
    distance = 1
    while distance < size:
        value = value + swap(value, axis, distance, size)
        distance *= 2
    return value


class Line:
    def __init__(self):
        self.piece, self.came, self.total, self.done = [], [], [], []

    def start(self, piece):
        k = len(self.piece)
        before = ((self.came, k - 1), (self.total, k - 2), (self.done, k - 3))
        earlier = [v[i] for v, i in before if i >= 0]
        if earlier:
            (piece,) = after([piece], *earlier)
        self.piece.append(piece)

    def land(self, *hold):
        piece = self.piece[len(self.came)]
        came = lax.ppermute(piece, "ctx", [(0, 1), (3, 2)])
        if hold:
            (came,) = after([came], *hold)
        self.came.append(came)
        inward = piece + came
        self.total.append(inward + lax.ppermute(inward, "ctx", [(1, 2), (2, 1)]))
        self.done.append(lax.ppermute(self.total[-1], "ctx", [(1, 0), (2, 3)]))

    def put(self, piece):
        self.start(piece)
        self.land()


def attend_kernel(
    heads, count, tiles, q, kv, q_code, q_base, k_code, mixed, lse, top, total, acc
):
    step = pl.program_id(0)
    top[...] = jnp.full_like(top, NEGATIVE)
    total[...] = jnp.zeros_like(total)
    acc[...] = jnp.zeros_like(acc)
    code, base = q_code[...], q_base[...]

    def body(j, carry):
        tile = tiles[step, j]
        keys = kv[tile, :HD]
        values = kv[tile, HD:]
        key_code = k_code[tile]
        allowed = (key_code <= code) & (key_code >= base)
        for h in range(heads):
            scores = jnp.where(allowed, dot(keys, q[h], 0, 0), NEGATIVE)
            before = top[h : h + 1]
            highest = jnp.maximum(before, jnp.max(scores, axis=0, keepdims=True))
            probs = jnp.exp(scores - highest)
            fade = jnp.exp(before - highest)
            top[h : h + 1] = highest
            total[h : h + 1] = total[h : h + 1] * fade + jnp.sum(probs, axis=0, keepdims=True)
            acc[h] = acc[h] * fade + dot(values, probs.astype(jnp.bfloat16), 1, 0)
        return carry

    lax.fori_loop(0, count[step], body, 0)
    sums = total[...]
    lse[...] = top[...] + jnp.log(sums)
    inverse = 1.0 / sums
    for h in range(heads):
        mixed[h] = acc[h] * inverse[h : h + 1]


def attend(count, tiles, q, kv, q_code, q_base, k_code):
    heads, _, rows = q.shape
    stack = pl.BlockSpec(kv.shape, lambda i, *_: (0, 0, 0))
    codes = pl.BlockSpec(k_code.shape, lambda i, *_: (0, 0, 0))
    line = pl.BlockSpec((1, TILE), lambda i, *_: (0, i))
    block = pl.BlockSpec((heads, HD, TILE), lambda i, *_: (0, 0, i))
    return pl.pallas_call(
        functools.partial(attend_kernel, heads),
        grid_spec=pltpu.PrefetchScalarGridSpec(
            num_scalar_prefetch=2,
            grid=(rows // TILE,),
            in_specs=[block, stack, line, line, codes],
            out_specs=[block, pl.BlockSpec((heads, TILE), lambda i, *_: (0, i))],
            scratch_shapes=[
                pltpu.VMEM((heads, TILE), jnp.float32),
                pltpu.VMEM((heads, TILE), jnp.float32),
                pltpu.VMEM((heads, HD, TILE), jnp.float32),
            ],
        ),
        out_shape=[
            jax.ShapeDtypeStruct((heads, HD, rows), jnp.float32),
            jax.ShapeDtypeStruct((heads, rows), jnp.float32),
        ],
        compiler_params=pltpu.CompilerParams(vmem_limit_bytes=60 * MIB),
        cost_estimate=SMALL,
    )(count, tiles, q, kv, q_code, q_base, k_code)


def attend_back_kernel(
    heads, count, tiles, q, kv, q_code, q_base, k_code, mixed, lse, upstream, dq, dkv, centre
):
    step = pl.program_id(0)

    @pl.when(step == 0)
    def _():
        dkv[...] = jnp.zeros_like(dkv)

    dq[...] = jnp.zeros_like(dq)
    code, base = q_code[...], q_base[...]
    for h in range(heads):
        centre[h : h + 1] = jnp.sum(
            mixed[h] * upstream[h].astype(jnp.float32), axis=0, keepdims=True
        )

    def body(j, carry):
        tile = tiles[step, j]
        keys = kv[tile, :HD]
        values = kv[tile, HD:]
        key_code = k_code[tile]
        allowed = (key_code <= code) & (key_code >= base)
        all_probs, all_scores = [], []
        for h in range(heads):
            scores = dot(keys, q[h], 0, 0) - lse[h : h + 1]
            probs = jnp.exp(jnp.where(allowed, scores, NEGATIVE))
            grad_probs = dot(values, upstream[h], 0, 0)
            grad_scores = (probs * (grad_probs - centre[h : h + 1])).astype(jnp.bfloat16)
            all_probs.append(probs.astype(jnp.bfloat16))
            all_scores.append(grad_scores)
            dq[h] += dot(keys, grad_scores, 1, 0)
        join = lambda parts: jnp.concatenate(parts, axis=1)
        every = range(heads)
        dkv[tile, :HD] += dot(join([q[h] for h in every]), join(all_scores), 1, 1)
        dkv[tile, HD:] += dot(join([upstream[h] for h in every]), join(all_probs), 1, 1)
        return carry

    lax.fori_loop(0, count[step], body, 0)


def attend_back(count, tiles, q, kv, q_code, q_base, k_code, mixed, lse, upstream):
    heads, _, rows = q.shape
    stack = pl.BlockSpec(kv.shape, lambda i, *_: (0, 0, 0))
    codes = pl.BlockSpec(k_code.shape, lambda i, *_: (0, 0, 0))
    line = pl.BlockSpec((1, TILE), lambda i, *_: (0, i))
    block = pl.BlockSpec((heads, HD, TILE), lambda i, *_: (0, 0, i))
    return pl.pallas_call(
        functools.partial(attend_back_kernel, heads),
        grid_spec=pltpu.PrefetchScalarGridSpec(
            num_scalar_prefetch=2,
            grid=(rows // TILE,),
            in_specs=[
                block,
                stack,
                line,
                line,
                codes,
                block,
                pl.BlockSpec((heads, TILE), lambda i, *_: (0, i)),
                block,
            ],
            out_specs=[block, stack],
            scratch_shapes=[pltpu.VMEM((heads, TILE), jnp.float32)],
        ),
        out_shape=[
            jax.ShapeDtypeStruct((heads, HD, rows), jnp.float32),
            jax.ShapeDtypeStruct(kv.shape, jnp.float32),
        ],
        compiler_params=pltpu.CompilerParams(vmem_limit_bytes=60 * MIB),
        cost_estimate=cost(24),
    )(count, tiles, q, kv, q_code, q_base, k_code, mixed, lse, upstream)


def plan_tiles(q_code, q_base, k_code):
    rows, keys = q_code.shape[0], k_code.shape[0]
    allowed = (k_code[None, :] <= q_code[:, None]) & (k_code[None, :] >= q_base[:, None])
    used = jnp.any(allowed.reshape(rows // TILE, TILE, keys // TILE, TILE), axis=(1, 3))
    place = jnp.cumsum(used.astype(jnp.int32), axis=1) - 1
    ladder = jnp.arange(keys // TILE)
    hit = used[:, :, None] & (place[:, :, None] == ladder[None, None, :])
    tiles = jnp.sum(jnp.where(hit, ladder[None, :, None], 0), axis=1).astype(jnp.int32)
    return jnp.sum(used.astype(jnp.int32), axis=1), tiles


def nothing(*refs):
    pass


def after(values, *tokens):
    anywhere = pl.BlockSpec(memory_space=pl.ANY)
    return pl.pallas_call(
        nothing,
        in_specs=[anywhere] * (len(values) + len(tokens)),
        out_specs=[anywhere] * len(values),
        out_shape=[jax.ShapeDtypeStruct(v.shape, v.dtype) for v in values],
        input_output_aliases={i: i for i in range(len(values))},
    )(*values, *tokens)


def outer_kernel(parts, places, upstream, *refs):
    pieces, out = refs[:parts], refs[parts]
    total = 0.0
    for i in range(parts):
        columns = pl.ds(pl.multiple_of(places[i], TILE), pieces[i].shape[1])
        total = total + dot(upstream[:, columns], pieces[i][...], 1, 1)
    out[...] = total


def outer(places, upstream, down_w):
    count, width = upstream.shape
    units = down_w[0].shape[0]
    block = 256
    flat = [pl.BlockSpec((block, w.shape[1]), lambda i, *_: (i, 0)) for w in down_w]
    return pl.pallas_call(
        functools.partial(outer_kernel, len(down_w)),
        grid_spec=pltpu.PrefetchScalarGridSpec(
            num_scalar_prefetch=1,
            grid=(pl.cdiv(units, block),),
            in_specs=[pl.BlockSpec((count, width), lambda i, *_: (0, 0)), *flat],
            out_specs=pl.BlockSpec((count, block), lambda i, *_: (0, i)),
        ),
        out_shape=jax.ShapeDtypeStruct((count, units), jnp.float32),
        compiler_params=pltpu.CompilerParams(vmem_limit_bytes=60 * MIB),
        cost_estimate=SMALL,
    )(places, upstream, *down_w)


def middle_kernel(parts, places, rows, grads, *refs):
    pieces, (hidden, dgate, dupper) = refs[: 2 * parts], refs[2 * parts :]
    gate = upper = 0.0
    for i in range(parts):
        columns = pl.ds(pl.multiple_of(places[i], TILE), pieces[i].shape[0])
        left = rows[:, columns]
        gate = gate + dot(left, pieces[i][...], 1, 0)
        upper = upper + dot(left, pieces[parts + i][...], 1, 0)
    grad = grads[...]
    sigma = 1.0 / (1.0 + jnp.exp(-gate))
    swish = gate * sigma
    hidden[...] = (swish * upper).astype(jnp.bfloat16)
    dgate[...] = (grad * upper * sigma * (1.0 + gate * (1.0 - sigma))).astype(jnp.bfloat16)
    dupper[...] = (grad * swish).astype(jnp.bfloat16)


def middle(places, rows, grads, gate_w, upper_w):
    parts = len(gate_w)
    count, width = rows.shape
    units = gate_w[0].shape[1]
    block = 384 if units % 384 == 0 else 256
    out = pl.BlockSpec((count, block), lambda i, *_: (0, i))
    tall = [pl.BlockSpec((w.shape[0], block), lambda i, *_: (0, i)) for w in gate_w]
    return pl.pallas_call(
        functools.partial(middle_kernel, parts),
        grid_spec=pltpu.PrefetchScalarGridSpec(
            num_scalar_prefetch=1,
            grid=(pl.cdiv(units, block),),
            in_specs=[pl.BlockSpec((count, width), lambda i, *_: (0, 0)), out, *tall, *tall],
            out_specs=[out, out, out],
        ),
        out_shape=[jax.ShapeDtypeStruct((count, units), jnp.bfloat16)] * 3,
        compiler_params=pltpu.CompilerParams(vmem_limit_bytes=60 * MIB),
        cost_estimate=cost(9),
    )(places, rows, grads, *gate_w, *upper_w)


def project_kernel(parts, factors, steps, over_left, over_right, skip, places, *refs):
    lefts, pieces, out = refs[:factors], refs[factors:-1], refs[-1]
    step = pl.program_id(0)

    def one(i, start):
        total = 0.0
        for f in range(factors):
            left, right = lefts[f], pieces[f * parts + i]
            left = left[:, start:] if over_left else left[start:]
            right = right[:, start:] if over_right else right[start:]
            total = total + dot(left, right, over_left, over_right)
        out[...] = total.astype(out.dtype)

    for i in range(parts):
        here = (step >= i * steps) & (step < (i + 1) * steps)
        if skip:
            pl.when(here & (places[parts] == 0))(functools.partial(one, i, 0))
            pl.when(here & (places[parts] != 0))(functools.partial(one, i, skip))
        else:
            pl.when(here)(functools.partial(one, i, 0))


def project(places, lefts, weights, over_left, over_right, skip=0):
    parts, factors = len(weights[0]), len(lefts)
    axis = 1 - over_right
    size = weights[0][0].shape[axis]
    block = min(512, size)
    steps = size // block
    depth = weights[0][0].shape[over_right]
    count = lefts[0].shape[1 - over_left]

    def spec(i):
        at = lambda s: jnp.clip(s - i * steps, 0, steps - 1)
        if axis == 0:
            return pl.BlockSpec((block, depth), lambda s, *_: (at(s), 0))
        return pl.BlockSpec((depth, block), lambda s, *_: (0, at(s)))

    return pl.pallas_call(
        functools.partial(
            project_kernel, parts, factors, steps, over_left, over_right, skip
        ),
        grid_spec=pltpu.PrefetchScalarGridSpec(
            num_scalar_prefetch=1,
            grid=(parts * steps,),
            in_specs=[pl.BlockSpec(v.shape, lambda s, *_: (0, 0)) for v in lefts]
            + [spec(i) for _ in range(factors) for i in range(parts)],
            out_specs=pl.BlockSpec(
                (count, block), lambda s, p: (0, p[s // steps] // block + s % steps)
            ),
        ),
        out_shape=jax.ShapeDtypeStruct((count, parts * size), jnp.bfloat16),
        compiler_params=pltpu.CompilerParams(vmem_limit_bytes=60 * MIB),
        cost_estimate=cost(3 * len(lefts)),
    )(places, *lefts, *[w for weight in weights for w in weight])


def collect_kernel(parts, sets, places, *refs):
    rows, pieces, out = refs[:sets], refs[sets:-1], refs[-1]
    at = 0
    for block in rows:
        total = 0.0
        for i in range(parts):
            columns = pl.ds(pl.multiple_of(places[i], TILE), pieces[i].shape[1])
            total = total + dot(pieces[i][...], block[:, columns], 1, 1)
        out[:, at : at + block.shape[0]] = total.astype(out.dtype)
        at += block.shape[0]


def collect(places, rows, pieces):
    parts, count = len(pieces), sum(v.shape[0] for v in rows)
    units = pieces[0].shape[0]
    block = 256
    specs = [pl.BlockSpec((block, w.shape[1]), lambda i, *_: (i, 0)) for w in pieces]
    return pl.pallas_call(
        functools.partial(collect_kernel, parts, len(rows)),
        grid_spec=pltpu.PrefetchScalarGridSpec(
            num_scalar_prefetch=1,
            grid=(units // block,),
            in_specs=[pl.BlockSpec(v.shape, lambda i, *_: (0, 0)) for v in rows] + specs,
            out_specs=pl.BlockSpec((block, count), lambda i, *_: (i, 0)),
        ),
        out_shape=jax.ShapeDtypeStruct((units, count), jnp.bfloat16),
        compiler_params=pltpu.CompilerParams(vmem_limit_bytes=60 * MIB),
        cost_estimate=cost(5),
    )(places, *rows, *pieces)


def weigh_kernel(parts, at_left, at_right, wide, places, *refs):
    lefts, rights, out = refs[:parts], refs[parts:-1], refs[-1]
    columns = pl.ds(pl.multiple_of(places[at_right], TILE), wide)
    total = 0.0
    for left, right in zip(lefts, rights):
        total = total + dot(left[...], right[:, columns], 0, 0)
    out[...] = total.astype(out.dtype)


def weigh(places, lefts, at_left, tall, rights, at_right, wide):
    parts = len(lefts)
    count = lefts[0].shape[0]
    block = TILE if tall % 256 or lefts[0].shape[1] % 256 else 256
    if tall % 512 == 0 and lefts[0].shape[1] % 512 == 0:
        block = 512
    return pl.pallas_call(
        functools.partial(weigh_kernel, parts, at_left, at_right, wide),
        grid_spec=pltpu.PrefetchScalarGridSpec(
            num_scalar_prefetch=1,
            grid=(tall // block,),
            in_specs=[
                pl.BlockSpec((count, block), lambda i, p: (0, p[at_left] // block + i))
                for _ in lefts
            ]
            + [pl.BlockSpec(v.shape, lambda i, p: (0, 0)) for v in rights],
            out_specs=pl.BlockSpec((block, wide), lambda i, p: (i, 0)),
        ),
        out_shape=jax.ShapeDtypeStruct((tall, wide), jnp.bfloat16),
        compiler_params=pltpu.CompilerParams(vmem_limit_bytes=60 * MIB),
        cost_estimate=cost(6),
    )(places, *lefts, *rights)


def plus_kernel(left, right, out):
    out[...] = (left[...].astype(jnp.float32) + right[...].astype(jnp.float32)).astype(out.dtype)


def plus(left, right):
    rows, width = left.shape
    block = rows // 4 if rows % 64 == 0 else rows
    spec = pl.BlockSpec((block, width), lambda i: (i, 0))
    return pl.pallas_call(
        plus_kernel,
        grid=(rows // block,),
        in_specs=[spec, spec],
        out_specs=spec,
        out_shape=jax.ShapeDtypeStruct(left.shape, left.dtype),
        compiler_params=pltpu.CompilerParams(vmem_limit_bytes=60 * MIB),
        cost_estimate=SMALL,
    )(left, right)


def entry_kernel(parts, query_steps, places, rows, cosine, sine, *refs):
    pieces, (q, kv) = refs[:parts], refs[parts:]
    step = pl.program_id(0)
    total = 0.0
    for i in range(parts):
        columns = pl.ds(pl.multiple_of(places[i], TILE), pieces[i].shape[0])
        total = total + dot(pieces[i][...], rows[:, columns], 0, 1)
    half = HD // 2

    def turned(start):
        former, latter = total[start : start + half], total[start + half : start + HD]
        return jnp.concatenate(
            [
                former * cosine[...] - latter * sine[...],
                latter * cosine[...] + former * sine[...],
            ],
            axis=0,
        ).astype(jnp.bfloat16)

    @pl.when(step < query_steps)
    def _():
        for start in (0, HD):
            q[start : start + HD] = turned(start) * 0.125

    @pl.when(step == query_steps)
    def _():
        keys = turned(0)
        values = total[HD:].astype(jnp.bfloat16)
        for j in range(kv.shape[0]):
            columns = slice(j * TILE, (j + 1) * TILE)
            kv[j, :HD] = keys[:, columns]
            kv[j, HD:] = values[:, columns]


def entry(places, rows, cosine, sine, pieces):
    parts = len(pieces)
    count, width = rows.shape
    steps = pieces[0].shape[1] // TILE - 1
    table = pl.BlockSpec(cosine.shape, lambda i, *_: (0, 0))
    return pl.pallas_call(
        functools.partial(entry_kernel, parts, steps),
        grid_spec=pltpu.PrefetchScalarGridSpec(
            num_scalar_prefetch=1,
            grid=(steps + 1,),
            in_specs=[pl.BlockSpec((count, width), lambda i, *_: (0, 0)), table, table]
            + [pl.BlockSpec((w.shape[0], TILE), lambda i, *_: (0, i)) for w in pieces],
            out_specs=[
                pl.BlockSpec((TILE, count), lambda i, *_: (jnp.minimum(i, steps - 1), 0)),
                pl.BlockSpec((count // TILE, TILE, TILE), lambda i, *_: (0, 0, 0)),
            ],
        ),
        out_shape=[
            jax.ShapeDtypeStruct((steps * TILE, count), jnp.bfloat16),
            jax.ShapeDtypeStruct((count // TILE, TILE, TILE), jnp.bfloat16),
        ],
        compiler_params=pltpu.CompilerParams(vmem_limit_bytes=60 * MIB),
        cost_estimate=SMALL,
    )(places, rows, cosine, sine, *pieces)


def place_kernel(order, first, second, out):
    step = pl.program_id(0)

    @pl.when(step < 2)
    def _():
        out[...] = first[...].astype(out.dtype)

    @pl.when(step >= 2)
    def _():
        out[...] = second[...].astype(out.dtype)


def place(order, halves, dtype):
    size, width = halves[0].shape[0] // 2, halves[0].shape[1]
    return pl.pallas_call(
        place_kernel,
        grid_spec=pltpu.PrefetchScalarGridSpec(
            num_scalar_prefetch=1,
            grid=(4,),
            in_specs=[
                pl.BlockSpec((size, width), lambda i, *_: (jnp.minimum(i, 1), 0)),
                pl.BlockSpec((size, width), lambda i, *_: (jnp.maximum(i - 2, 0), 0)),
            ],
            out_specs=pl.BlockSpec((size, width), lambda i, o: (o[i], 0)),
        ),
        out_shape=jax.ShapeDtypeStruct((4 * size, width), dtype),
        compiler_params=pltpu.CompilerParams(vmem_limit_bytes=60 * MIB),
        cost_estimate=cost(5),
    )(order, *halves)


def finish_kernel(axis, where, kept, *refs):
    out = refs[-1]
    if len(refs) == 1:
        out[...] = kept[...].astype(jnp.float32)
        return
    came = jnp.where(where[0] != 0, refs[0][...], refs[1][...])
    for i, piece in enumerate((kept[...], came)):
        at = pl.ds(pl.multiple_of(where[1 + i], TILE), piece.shape[axis])
        if axis == 0:
            out[at] = piece.astype(jnp.float32)
        else:
            out[:, at] = piece.astype(jnp.float32)


def finish(where, axis, kept, *came):
    shape = list(kept.shape)
    shape[axis] += came[0].shape[axis] if came else 0
    block = 256 if shape[1 - axis] % 256 == 0 else shape[1 - axis]

    def spec(size):
        if axis == 0:
            return pl.BlockSpec((size, block), lambda s, *_: (0, s))
        return pl.BlockSpec((block, size), lambda s, *_: (s, 0))

    return pl.pallas_call(
        functools.partial(finish_kernel, axis),
        grid_spec=pltpu.PrefetchScalarGridSpec(
            num_scalar_prefetch=1,
            grid=(shape[1 - axis] // block,),
            in_specs=[spec(p.shape[axis]) for p in (kept, *came)],
            out_specs=spec(shape[axis]),
        ),
        out_shape=jax.ShapeDtypeStruct(shape, jnp.float32),
        compiler_params=pltpu.CompilerParams(vmem_limit_bytes=60 * MIB),
        cost_estimate=cost(6),
    )(where, kept, *came)


def rms_scale(values):
    return lax.rsqrt(jnp.mean(values * values, axis=-1, keepdims=True) + epsilon)


def norm_back(values, scale, gain, upstream):
    weighted = upstream * gain
    return scale * weighted - values * scale**3 * jnp.mean(
        values * weighted, axis=-1, keepdims=True
    )


def turn(values, cosine, sine):
    half = HD // 2
    former, latter = values[:, :half], values[:, half:]
    return jnp.concatenate(
        [former * cosine - latter * sine, latter * cosine + former * sine], axis=1
    )


def per_device(
    sizes,
    tokens,
    first_gain,
    query_weight,
    keyval_weight,
    output_weight,
    second_gain,
    gate_weight,
    up_weight,
    down_weight,
    segment_ids,
    positions,
    cotangent,
):
    nx, nz, nt = sizes
    low, high = jnp.bfloat16, jnp.float32
    rows, width = tokens.shape
    block = rows // nt
    half = width // nx
    here_x, here_z, here_t = (lax.axis_index(a) for a in ("fsdp", "ctx", "tp"))
    paired = nx == 2
    assert nt == 4 and block % TILE == 0 and keyval_weight.shape[1] == 2 * HD
    order = jnp.stack([here_t ^ k for k in ORDER]).astype(jnp.int32)

    def arranged(whole, axis=0):
        return jnp.concatenate(
            [
                lax.dynamic_slice_in_dim(whole, (here_t ^ k) * block, block, axis)
                for k in ORDER
            ],
            axis=axis,
        )

    def part(whole, start, size, axis):
        return lax.dynamic_slice_in_dim(whole, start, size, axis)

    def mine(whole):
        return part(whole, here_x * half, half, 1)

    def theirs(whole):
        return part(whole, (1 - here_x) * half, half, 1)

    units = gate_weight.shape[1]
    query_width = query_weight.shape[1]
    heads = query_width // HD
    qkv_shard = jnp.concatenate([query_weight, keyval_weight], axis=1)
    gain_shards = jnp.stack([first_gain, second_gain])
    if paired:
        big = (units // TILE + 1) // 2 * TILE
        small = units - big
        spare = big - small
        places = jnp.stack(
            [here_x * half, (1 - here_x) * half, here_x, 0 * here_x, here_x * spare]
        ).astype(jnp.int32)
        at, at_theirs = here_x * small, (1 - here_x) * small
        gains_there = over_x(gain_shards)
        gains = jnp.where(
            here_x == 0,
            jnp.concatenate([gain_shards, gains_there], axis=1),
            jnp.concatenate([gains_there, gain_shards], axis=1),
        )
        qkv_w = (qkv_shard, over_x(qkv_shard))
        output_w = (output_weight, over_x(after([output_weight], gains_there)[0]))
        fourth = half // nz

        def around(received):
            return lax.all_gather(received, "ctx", axis=0, tiled=True)

        def columns(weight):
            start = (here_z * fourth, at_theirs)
            piece = lax.dynamic_slice(weight, start, (fourth, big))
            return over_x(after([piece], gains_there)[0])

        gate_fourth, upper_fourth = columns(gate_weight), columns(up_weight)
        gate_own, upper_own = part(gate_weight, at, big, 1), part(up_weight, at, big, 1)
        down_w = (part(down_weight, at, big, 0), over_x(part(down_weight, at_theirs, big, 0)))
    else:
        spare = 0
        places = jnp.zeros((2,), jnp.int32)
        whole = lambda shard, dim: lax.all_gather(shard, "fsdp", axis=dim, tiled=True)
        gains = whole(gain_shards, 1)
        qkv_w, output_w = (whole(qkv_shard, 0),), (whole(output_weight, 1),)
        gate_w, upper_w = (whole(gate_weight, 0),), (whole(up_weight, 0),)
        down_w = (whole(down_weight, 1),)
    gains = gains.astype(high)
    gain_one, gain_two = gains[0], gains[1]

    codes = arranged((segment_ids * CODE + positions).reshape(nz, rows), 1)
    bases = arranged((segment_ids * CODE).reshape(nz, rows), 1)
    q_code = lax.dynamic_index_in_dim(codes, here_z, 0, False)
    q_base = lax.dynamic_index_in_dim(bases, here_z, 0, False)
    k_code = jnp.concatenate(
        [
            lax.dynamic_index_in_dim(codes, (here_z + nz - d) % nz, 0, False)
            for d in range(nz)
        ]
    )
    count, tiles = plan_tiles(q_code, q_base, k_code)
    k_wide = jnp.broadcast_to(k_code.reshape(-1, TILE, 1), (nz * rows // TILE, TILE, TILE))
    masks = (q_code[None], q_base[None], k_wide)
    spots = (q_code - q_base).astype(high)
    freqs = jnp.exp(jnp.arange(HD // 2).astype(high) * (-2.0 * math.log(10000.0) / HD))
    angles = freqs[:, None] * spots[None, :]
    cosine, sine = jnp.cos(angles), jnp.sin(angles)

    tokens = arranged(tokens)
    cotangent = arranged(cotangent)
    inputs = tokens.astype(high)
    scale_one = rms_scale(inputs)
    normed_one = (inputs * scale_one * gain_one).astype(low)
    q, kv = entry(places, normed_one, cosine, sine, qkv_w)
    q = q.reshape(heads, HD, rows)
    kv = jnp.concatenate([kv] + [shift(kv, "ctx", nz, d) for d in range(1, nz)], axis=0)
    mixed, lse = attend(count, tiles, q, kv, *masks)
    if paired:
        gate_fourth, upper_fourth = after([gate_fourth, upper_fourth], lse)
        gate_w = (gate_own, around(gate_fourth))
        upper_w = (upper_own, around(upper_fourth))

    mixed_low = mixed.reshape(query_width, rows).astype(low)
    attn = project(places, [mixed_low], [output_w], 0, 0)
    keep, give = cut(attn[None], 1)
    attn_own, _ = scatter_rows(keep, give)
    one_own = inputs[:block] + attn_own
    scale_two = rms_scale(one_own)
    normed_own = (one_own * scale_two * gain_two).astype(low)

    if paired:
        there = over_x(cotangent[:block])
        there = jnp.concatenate([there, over_y(there)], axis=0)
        upstream = [
            jnp.concatenate([c, t], axis=0)
            for c, t in zip(jnp.split(cotangent, 2), (there, over_core(there)))
        ]
        (normed_own,) = after([normed_own], *upstream, down_w[1], gate_w[1])
        grads = [outer(places, u, down_w) for u in upstream]
        normed_two = gather_pair(normed_own, [grads[0]], [grads[1], upper_w[1]])
    else:
        normed_two = gather_own(normed_own)
        upstream = jnp.split(cotangent, 2)
        grads = [outer(places, u, down_w) for u in upstream]
    normed_two = [v.reshape(-1, width) for v in normed_two]
    sets = 2 if paired else 1

    def spread(value, dim):
        return lax.psum_scatter(value, "fsdp", scatter_dimension=dim, tiled=True)

    def forward(i):
        return middle(places, normed_two[i], grads[i], gate_w, upper_w)

    def back(i):
        made = project(places, [dgate[i], dupper[i]], [gate_w, upper_w], 1, 1, spare)
        return made.reshape(sets, -1, width)

    def ffn(i):
        return project(places, [hidden[i]], [down_w], 1, 0, spare).reshape(sets, -1, width)

    line = Line()
    scattered, sums = {}, {}

    def scatter(name, piece):
        scattered[name] = lax.psum_scatter(piece, "ctx", scatter_dimension=0, tiled=True)

    def gather(name, *tokens):
        piece = scattered[name]
        if tokens:
            (piece,) = after([piece], *tokens)
        sums[name] = lax.all_gather(piece, "ctx", axis=0, tiled=True)

    hidden, dgate, dupper = [None, None], [None, None], [None, None]
    if paired:
        hidden[1], dgate[1], dupper[1] = forward(1)
        (places,) = after([places], hidden[1])
        grad_give = back(1)
        (places,) = after([places], grad_give)
        hidden[0], dgate[0], dupper[0] = forward(0)
        (places,) = after([places], hidden[0])
        kept_down = weigh(places, hidden, 3, big, upstream, 0, half)
        scatter("down", kept_down)
        (places,) = after([places], kept_down)
        grad_keep = back(0)
        kept = {}

        def between(sent):
            after_sent = after([places], grad_keep, *sent)[0]
            kept["gate"] = weigh(after_sent, normed_two, 0, half, dgate, 3, big)
            scatter("gate", kept["gate"])
            return [kept["gate"]]

        grad_own, sent = scatter_rows(grad_keep, grad_give, between)
        (places,) = after([places], kept["gate"], *sent)
        given_down = weigh(places, hidden, 4, small, upstream, 1, half)
        (places,) = after([places], given_down)
        (grad_own,) = after([grad_own], given_down)
    else:
        for i in range(2):
            hidden[i], dgate[i], dupper[i] = forward(i)
        weight_grad = lambda lefts, rights: sum(
            dot(left, right, 0, 0) for left, right in zip(lefts, rights)
        ).astype(low)
        scatter("down", spread(weight_grad(hidden, upstream), 1))
        scatter("gate", spread(weight_grad(normed_two, dgate), 0))
        scatter("upper", spread(weight_grad(normed_two, dupper), 0))
        grad_own, _ = scatter_rows(back(0), back(1))
    grad_one = cotangent[:block].astype(high) + norm_back(
        one_own, scale_two, gain_two, grad_own
    )
    grad_one_low = grad_one.astype(low)
    gain_two_sum = jnp.sum(grad_own * one_own * scale_two, axis=0)
    grad_attn = gather_own(grad_one_low)
    if paired:
        (places,) = after([places], grad_one_low)
        kept_upper = weigh(places, normed_two, 0, half, dupper, 3, big)
        scatter("upper", kept_upper)
        (places,) = after([places], kept_upper)
        given_gate = weigh(places, normed_two, 1, half, dgate, 4, small)
        (places,) = after([places], given_gate)
        line.put(over_x(given_down))
    grad_mixed = collect(places, grad_attn, output_w).reshape(heads, HD, rows)
    grad_attn = jnp.concatenate(grad_attn, axis=0)

    if paired:
        (grad_mixed,) = after([grad_mixed], line.piece[0], scattered["gate"])
    dq, dkv = attend_back(count, tiles, q, kv, *masks, mixed, lse, grad_mixed)
    per = rows // TILE
    dkv_own = dkv[:per]
    moved = [dkv[d * per : (d + 1) * per].astype(low) for d in range(1, nz)]
    received = [shift(m, "ctx", nz, nz - 1 - d) for d, m in enumerate(moved)]
    if paired:
        (places,) = after([places], *moved)
        given_upper = weigh(places, normed_two, 1, half, dupper, 4, small)
        (places,) = after([places], given_upper)
        came_gate = over_x(given_gate)
        line.start(came_gate)
        gather("down")
        received = after(received, given_upper, line.piece[1], scattered["upper"], sums["down"])
        gather("gate", scattered["upper"])
        came_upper = over_x(given_upper)
        attn_there, one_there, mixed_there = after(
            [theirs(grad_attn), theirs(normed_one), mixed_low], came_upper
        )
    else:
        line.put(spread(dot(mixed_low, grad_attn, 1, 0).astype(low), 1))
    for m in received:
        dkv_own = dkv_own + m.astype(high)
    dkv_own = jnp.transpose(dkv_own, (1, 0, 2)).reshape(2 * HD, rows)
    dq = turn(dq * 0.125, cosine, -sine).reshape(query_width, rows)
    dk = turn(dkv_own[None, :HD], cosine, -sine)[0]
    dqkv = jnp.concatenate([dq, dk, dkv_own[HD:]], axis=0).astype(low)
    first = project(places, [dqkv], [qkv_w], 0, 1)
    (places,) = after([places], first)
    keep, give = cut(first[None], 1)
    first_own, sent = scatter_rows(keep, give)
    if paired:
        line.land(first_own)
        line.put(came_upper)
        gather("upper", *sent)
        (places,) = after([places], *sent)
    else:
        qkv_grad = spread(dot(normed_one, dqkv, 0, 1).astype(low), 0)
    scale_own = scale_one[:block]
    inputs_own = inputs[:block]
    gain_one_sum = jnp.sum(first_own * inputs_own * scale_own, axis=0)
    input_own = grad_one + norm_back(inputs_own, scale_own, gain_one, first_own)
    input_low = input_own.astype(low)
    if paired:
        attn_there, mixed_there, one_there = after(
            [attn_there, mixed_there, one_there], input_low
        )
        attn_there, one_there = both_cores(attn_there), both_cores(one_there)
        mixed_there = over_x(mixed_there)
        output_grad = dot(mixed_low, mine(grad_attn), 1, 0) + dot(
            mixed_there, attn_there, 1, 0
        )
        line.put(output_grad.astype(low))
        (dqkv_there,) = after([over_x(dqkv)], input_low)
        qkv_grad = (
            dot(mine(normed_one), dqkv, 0, 1) + dot(one_there, dqkv_there, 0, 1)
        ).astype(low)
    if not paired:
        gather("down")
        gather("gate")
        gather("upper")
    late = [line.piece[2]] if paired else []
    (places,) = after([places], input_low)
    if paired:
        (places,) = after([places], sums["gate"])
    input_grad = place(order, gather_own(input_low, *late), high)
    ffn_give = ffn(1)
    if paired:
        (places,) = after([places], ffn_give, sums["upper"])
    ffn_own, _ = scatter_rows(ffn(0), ffn_give)
    activations = place(order, gather_own((one_own + ffn_own).astype(low)), low)

    gain_sums = sum_all(jnp.stack([gain_one_sum, gain_two_sum]), "tp", nt)
    if paired:
        gain_sums = mine(gain_sums) + over_x(theirs(gain_sums))
    else:
        gain_sums = lax.psum_scatter(gain_sums, "fsdp", scatter_dimension=1, tiled=True)
    upper_half, lower_half = jnp.split(qkv_grad, 2)
    line.put(upper_half)
    long = lower_half.shape[1]
    extra = -(-gain_sums.size // (16 * long)) * 16
    gain_sums = jnp.pad(gain_sums.reshape(-1), (0, extra * long - gain_sums.size))
    gain_sums = gain_sums.reshape(extra, long).astype(low)
    line.put(jnp.concatenate([lower_half, gain_sums], axis=0))
    assert nz == 4
    inner = ((here_z == 1) | (here_z == 2)).astype(jnp.int32)
    if paired:
        where = jnp.stack([inner, here_x * small, (1 - here_x) * big]).astype(jnp.int32)
    else:
        where = jnp.stack([inner, 0, 0]).astype(jnp.int32)
    def whole(i):
        return jnp.where(inner != 0, line.total[i], line.done[i])

    down_grad, gate_grad, upper_grad = (
        finish(where, axis, sums[name], *([line.total[i], line.done[i]] if paired else []))
        for i, (name, axis) in enumerate((("down", 0), ("gate", 1), ("upper", 1)))
    )
    output_grad = whole(-3).astype(high)
    halves = (whole(-2).astype(high), whole(-1)[:-extra].astype(high))
    query_grad = jnp.concatenate([v[:, :query_width] for v in halves], axis=0)
    keyval_grad = jnp.concatenate([v[:, query_width:] for v in halves], axis=0)
    gain_sums = whole(-1)[-extra:].astype(high).reshape(-1)[: 2 * half].reshape(2, half)
    return (
        activations,
        input_grad,
        gain_sums[0],
        query_grad,
        keyval_grad,
        output_grad,
        gain_sums[1],
        gate_grad,
        upper_grad,
        down_grad,
    )


def solution(mesh):
    placed = (
        P(("fsdp", "ctx"), None),
        P("fsdp"),
        P("fsdp", "tp"),
        P("fsdp", "tp"),
        P("tp", "fsdp"),
        P("fsdp"),
        P("fsdp", "tp"),
        P("fsdp", "tp"),
        P("tp", "fsdp"),
        P("fsdp"),
        P("fsdp"),
        P(("fsdp", "ctx"), None),
    )
    sizes = (mesh.shape["fsdp"], mesh.shape["ctx"], mesh.shape["tp"])
    return jax.shard_map(
        functools.partial(per_device, sizes),
        mesh=mesh,
        in_specs=placed,
        out_specs=(
            P(("fsdp", "ctx"), None),
            P(("fsdp", "ctx"), None),
            P("fsdp"),
            P("fsdp", "tp"),
            P("fsdp", "tp"),
            P("tp", "fsdp"),
            P("fsdp"),
            P("fsdp", "tp"),
            P("fsdp", "tp"),
            P("tp", "fsdp"),
        ),
        check_vma=False,
    )
```
